128 devices in a mesh: kvp: 16 (over y, x), head: 8 (over z, core).
Axes of the slice: x: 4, y: 4, z: 4, core: 2. Of those that a mesh axis runs over, the one named last changes fastest.
Arguments:
- hidden_in: bfloat16 [64, 8192], P(None, 'kvp'), may hold values from -32 to 32
- norm_gain: bfloat16 [8192], P('kvp'), may hold values from 0.25 to 1.75
- w_query: bfloat16 [8192, 8192], P('kvp', 'head'), may hold values from -0.0625 to 0.0625
- w_key: bfloat16 [8192, 1024], P('kvp', 'head'), may hold values from -0.375 to 0.375
- w_value: bfloat16 [8192, 1024], P('kvp', 'head'), may hold values from -0.0625 to 0.0625
- w_out: bfloat16 [8192, 8192], P('head', 'kvp'), may hold values from -0.0625 to 0.0625
- post_gain: bfloat16 [8192], P('kvp'), may hold values from 0.25 to 1.75
- w_gate: bfloat16 [8192, 28672], P('kvp', 'head'), may hold values from -0.0625 to 0.0625
- w_up: bfloat16 [8192, 28672], P('kvp', 'head'), may hold values from -0.0625 to 0.0625
- w_down: bfloat16 [28672, 8192], P('head', 'kvp'), may hold values from -0.03125 to 0.03125
- cache_keys: bfloat16 [2560, 128, 1024], P('kvp', None, 'head'), may hold values from -128 to 128
- cache_values: bfloat16 [2560, 128, 1024], P('kvp', None, 'head'), may hold values from -6 to 6
- context_len: int32 [16], replicated, may hold values from 3969 to 28672, as said below
- slot_request: int32 [2560], P('kvp'), may hold values from -1 to 15, as said below
- slot_start: int32 [2560], P('kvp'), may hold values from 0 to 28544, as said below
Outputs:
- next_hidden: bfloat16 [64, 8192], P(None, 'kvp')
- draft_keys: bfloat16 [64, 1024], P(None, 'head')
- draft_values: bfloat16 [64, 1024], P(None, 'head')
The draws below stay inside these ranges and needn't reach their ends.
Inputs may be any that keep to these rules, and one draw needn't show every extreme that they name: Each request's cached tokens fill ceil(context_len / 128) blocks, between 32 and 224; the requests' blocks total 128 * 16. `slot_request`: every block of every request has exactly one slot. The 160 slots of a kvp device hold between 96 and 160 live blocks, which come first, and some device has all 160 live. A request's blocks stand in order in consecutive slots, continuing on the next kvp devices. `slot_start`: a multiple of 128; the slot holds tokens slot_start to slot_start + 127 of its request; 0 for empty slots.
All inputs are finite; a program needn't handle non-finite values.
Results may differ from the reference program's by a relative error of at most 0.017.
Values may be sent and summed in bfloat16 or wider, within the bound.
A program may use at most 128 MiB of HBM per device.

```python
import math
import jax
import jax.numpy as jnp
from jax import lax

D = 8192
H = 64
KVH = 8
HD = 128
FF = 28672
DRAFT = 4
BLOCK = 128
MEAN_BLK = 128
BLK_DEV = 160
LOW_DEV = 96
MIN_BLK = 32
MAX_BLK = 224
REQUESTS = 16
ROWS = 64
SLOTS = 2560


def plan_tables(key):
    req_key, dev_key, perm_key, dperm_key, off_key, order_key, force_key, dforce_key = jax.random.split(key, 8)
    half_count = REQUESTS // 2
    first_counts = jax.random.randint(req_key, (half_count,), MIN_BLK, MAX_BLK + 1)
    forced = jax.random.randint(force_key, (), 0, half_count)
    first_counts = jnp.where(jnp.arange(half_count, dtype=jnp.int32) == forced, MAX_BLK, first_counts)
    counts = jnp.concatenate([first_counts, 2 * MEAN_BLK - first_counts])
    counts = counts[jax.random.permutation(perm_key, REQUESTS)]
    first_loads = jax.random.randint(dev_key, (half_count,), LOW_DEV, BLK_DEV + 1)
    dforced = jax.random.randint(dforce_key, (), 0, half_count)
    first_loads = jnp.where(jnp.arange(half_count, dtype=jnp.int32) == dforced, BLK_DEV, first_loads)
    dev_loads = jnp.concatenate([first_loads, 2 * MEAN_BLK - first_loads])
    dev_loads = dev_loads[jax.random.permutation(dperm_key, REQUESTS)]
    offset = jax.random.randint(off_key, (REQUESTS,), 1, BLOCK + 1)
    offset = jnp.where(counts == MAX_BLK, BLOCK, jnp.where(counts == MIN_BLK, 1, offset))
    lengths = BLOCK * (counts - 1) + offset
    req_order = jax.random.permutation(order_key, REQUESTS)
    ordered = counts[req_order]
    req_end = jnp.cumsum(ordered)
    req_begin = req_end - ordered
    dev_end = jnp.cumsum(dev_loads)
    dev_begin = dev_end - dev_loads
    slot_index = jnp.arange(BLK_DEV, dtype=jnp.int32)
    global_block = dev_begin[:, None] + slot_index[None, :]
    live_slots = slot_index[None, :] < dev_loads[:, None]
    place_index = jnp.sum((global_block[..., None] >= req_end[None, None, :]).astype(jnp.int32), axis=-1)
    place_index = jnp.minimum(place_index, REQUESTS - 1)
    request = req_order[place_index]
    within = global_block - req_begin[place_index]
    slot_req = jnp.where(live_slots, request, -1).reshape(-1)
    slot_first = jnp.where(live_slots, within * BLOCK, 0).reshape(-1)
    return (lengths.astype(jnp.int32), slot_req.astype(jnp.int32), slot_first.astype(jnp.int32))


def draw_context_len(key, part):
    return plan_tables(key)[0]


def draw_slot_request(key, part):
    return plan_tables(key)[1]


def draw_slot_start(key, part):
    return plan_tables(key)[2]


def draw_hidden_in(key, part):
    key = jax.random.fold_in(key, 5)
    noise_key, row_key, col_key = jax.random.split(key, 3)
    row_scale = 10.0 ** jax.random.uniform(row_key, (ROWS, 1), minval=-0.5, maxval=0.5)
    col_spread = 10.0 ** jax.random.uniform(col_key, (1, D), minval=-0.5, maxval=0.5)
    ramp_cols = jnp.arange(D, dtype=jnp.float32)[None, :] / D - 0.5
    noise_draw = jax.random.normal(noise_key, (ROWS, D))
    rise_cols = 3.0 ** ramp_cols
    return jnp.clip(noise_draw * row_scale * col_spread * rise_cols, -32.0, 32.0).astype(jnp.bfloat16)


def draw_cache_keys(key, part):
    key = jax.random.fold_in(key, 7)
    noise_key = jax.random.fold_in(key, 0)
    cache_shape = (SLOTS, BLOCK, KVH * HD)
    values_out = 3.0 * jax.random.normal(noise_key, cache_shape)
    return jnp.clip(values_out, -128.0, 128.0).astype(jnp.bfloat16)


def steps_of(rng, shape, cuts, low, largest):
    gain, own = 1.0, jax.random.fold_in(rng, 6)
    for dim, parts in cuts:
        draws = jnp.exp(jax.random.uniform(jax.random.fold_in(own, dim), (parts,), jnp.float32, low / len(cuts), largest / len(cuts)))
        gain = gain * jnp.repeat(draws, shape[dim] // parts).reshape([-1 if axis == dim else 1 for axis in range(len(shape))])
    return gain


def noise(own_key, shape, width, limit, cuts=(), kind=jnp.bfloat16):
    values = width * jax.random.normal(own_key, shape, jnp.float32)
    if cuts:
        values = values * steps_of(own_key, shape, cuts, -0.22, 0.18)
    return jnp.clip(values, -limit, limit).astype(kind)


def setup_inputs(seed: int = 0) -> dict:
    arg_keys = jax.random.split(jax.random.key(seed), 16)
    hidden_in = draw_hidden_in(jax.random.fold_in(arg_keys[15], 71), 0)
    norm_gain = jnp.clip(1.0 + 0.15 * jax.random.normal(arg_keys[1], (D,), jnp.float32), 0.25, 1.75).astype(jnp.bfloat16)
    w_query = noise(arg_keys[2], (D, H * HD), D ** -0.5, 0.0625, ((0, 16), (1, 8)))
    w_key = noise(arg_keys[3], (D, KVH * HD), (D // 36) ** -0.5, 0.375, ((0, 16), (1, 8)))
    w_value = noise(arg_keys[4], (D, KVH * HD), D ** -0.5, 0.0625, ((0, 16), (1, 8)))
    w_out = noise(arg_keys[5], (H * HD, D), (H * HD) ** -0.5, 0.0625, ((0, 8), (1, 16)))
    post_gain = jnp.clip(1.0 + 0.15 * jax.random.normal(arg_keys[6], (D,), jnp.float32), 0.25, 1.75).astype(jnp.bfloat16)
    w_gate = noise(arg_keys[7], (D, FF), D ** -0.5, 0.0625, ((0, 16), (1, 8)))
    w_up = noise(arg_keys[8], (D, FF), D ** -0.5, 0.0625, ((0, 16), (1, 8)))
    w_down = noise(arg_keys[9], (FF, D), FF ** -0.5, 0.03125, ((0, 8), (1, 16)))
    cache_keys = draw_cache_keys(jax.random.fold_in(arg_keys[15], 71), 0)
    cache_values = noise(arg_keys[11], (SLOTS, BLOCK, KVH * HD), 1.0, 6.0, ((0, 16), (2, 8)))
    context_len = draw_context_len(jax.random.fold_in(arg_keys[15], 71), 0)
    slot_request = draw_slot_request(jax.random.fold_in(arg_keys[15], 71), 0)
    slot_start = draw_slot_start(jax.random.fold_in(arg_keys[15], 71), 0)
    return {"hidden_in": hidden_in, "norm_gain": norm_gain, "w_query": w_query, "w_key": w_key, "w_value": w_value, "w_out": w_out, "post_gain": post_gain, "w_gate": w_gate, "w_up": w_up, "w_down": w_down, "cache_keys": cache_keys, "cache_values": cache_values, "context_len": context_len, "slot_request": slot_request, "slot_start": slot_start}


EPSILON = 1e-05
THETA_BASE = 500000.0
FLOOR_SCORE = -1e+30

def rotate(vectors, positions):
    half_dim = vectors.shape[-1] // 2
    exponent = jnp.arange(half_dim, dtype=jnp.float32) * (2.0 / vectors.shape[-1])
    frequency = THETA_BASE ** (-exponent)
    angles = positions.astype(jnp.float32)[..., None, None] * frequency
    cosine = jnp.cos(angles)
    sine_part = jnp.sin(angles)
    first_half = vectors[..., :half_dim]
    second_half = vectors[..., half_dim:]
    return jnp.concatenate([first_half * cosine - second_half * sine_part, second_half * cosine + first_half * sine_part], axis=-1)

def reference(hidden_in, norm_gain, w_query, w_key, w_value, w_out, post_gain, w_gate, w_up, w_down, cache_keys, cache_values, context_len, slot_request, slot_start):
    groups = H // KVH
    query_rows = DRAFT * groups
    score_scale = 1.0 / math.sqrt(HD)
    hidden_f = hidden_in.astype(jnp.float32)
    mean_square = lax.optimization_barrier(jnp.mean(hidden_f * hidden_f, axis=1, keepdims=True))
    scaled_in = (hidden_f * norm_gain.astype(jnp.float32)).astype(jnp.bfloat16)
    inverse = lax.rsqrt(mean_square + EPSILON)
    query_raw = inverse * jnp.dot(scaled_in, w_query, preferred_element_type=jnp.float32)
    key_raw = inverse * jnp.dot(scaled_in, w_key, preferred_element_type=jnp.float32)
    value_raw = inverse * jnp.dot(scaled_in, w_value, preferred_element_type=jnp.float32)
    positions = context_len[:, None] + jnp.arange(DRAFT, dtype=jnp.int32)[None, :]
    queries = rotate(query_raw.reshape(REQUESTS, DRAFT, H, HD), positions).astype(jnp.bfloat16)
    draft_keys = rotate(key_raw.reshape(REQUESTS, DRAFT, KVH, HD), positions).astype(jnp.bfloat16)
    draft_values = value_raw.astype(jnp.bfloat16)
    grouped = queries.reshape(REQUESTS, DRAFT, KVH, groups, HD).transpose(0, 2, 1, 3, 4).reshape(REQUESTS, KVH, query_rows, HD)
    grouped_f = grouped.astype(jnp.float32)
    new_keys = draft_keys.transpose(0, 2, 1, 3).astype(jnp.float32)
    new_values = draft_values.reshape(REQUESTS, DRAFT, KVH, HD).transpose(0, 2, 1, 3).astype(jnp.float32)
    draft_scores = jnp.einsum('bkqd,bktd->bkqt', grouped_f, new_keys) * score_scale
    row_step = jnp.arange(query_rows, dtype=jnp.int32) // groups
    causal = jnp.arange(DRAFT, dtype=jnp.int32)[None, :] <= row_step[:, None]
    draft_scores = jnp.where(causal, draft_scores, FLOOR_SCORE)
    draft_max = lax.optimization_barrier(jnp.max(draft_scores, axis=-1))
    draft_weights = jnp.where(causal, jnp.exp(draft_scores - draft_max[..., None]), 0.0)
    draft_sum = lax.optimization_barrier(jnp.sum(draft_weights, axis=-1))
    draft_rounded = lax.optimization_barrier(draft_weights.astype(jnp.bfloat16)).astype(jnp.float32)
    draft_out = jnp.einsum('bkqt,bktd->bkqd', draft_rounded, new_values)
    slot_total = slot_request.shape[0]
    batch_slots = math.gcd(slot_total, 32)
    step_count = slot_total // batch_slots
    key_blocks = cache_keys.reshape(step_count, batch_slots, BLOCK, KVH, HD)
    value_blocks = cache_values.reshape(step_count, batch_slots, BLOCK, KVH, HD)
    request_blocks = slot_request.reshape(step_count, batch_slots)
    start_blocks = slot_start.reshape(step_count, batch_slots)
    request_ids = jnp.arange(REQUESTS, dtype=jnp.int32)
    token_offsets = jnp.arange(BLOCK, dtype=jnp.int32)

    def absorb(running, pieces):
        run_max, run_sum, run_out = running
        block_keys, block_values, block_req, block_start = pieces
        safe_req = jnp.clip(block_req, 0, REQUESTS - 1).astype(jnp.int32)
        chosen = grouped_f[safe_req]
        scores = jnp.einsum('skqd,stkd->skqt', chosen, block_keys.astype(jnp.float32)) * score_scale
        limits = context_len[safe_req]
        live_tokens = (block_req[:, None] >= 0) & (block_start[:, None] + token_offsets[None, :] < limits[:, None])
        live_mask = live_tokens[:, None, None, :]
        scores = jnp.where(live_mask, scores, FLOOR_SCORE)
        block_max = lax.optimization_barrier(jnp.max(scores, axis=-1))
        weights = jnp.where(live_mask, jnp.exp(scores - block_max[..., None]), 0.0)
        block_sum = lax.optimization_barrier(jnp.sum(weights, axis=-1))
        rounded = lax.optimization_barrier(weights.astype(jnp.bfloat16)).astype(jnp.float32)
        block_out = jnp.einsum('skqt,stkd->skqd', rounded, block_values.astype(jnp.float32))
        member = (block_req[:, None] == request_ids[None, :])[:, :, None, None]
        group_max = lax.optimization_barrier(jnp.max(jnp.where(member, block_max[:, None], FLOOR_SCORE), axis=0))
        new_max = jnp.maximum(run_max, group_max)
        factor = jnp.where(member, jnp.exp(block_max[:, None] - new_max[None]), 0.0)
        carried = jnp.exp(run_max - new_max)
        new_sum = run_sum * carried + lax.optimization_barrier(jnp.sum(factor * block_sum[:, None], axis=0))
        new_out = run_out * carried[..., None] + jnp.einsum('sbkq,skqd->bkqd', factor, block_out, precision=lax.Precision.HIGHEST)
        return ((new_max, new_sum, new_out), None)
    finals, _ = lax.scan(absorb, (draft_max, draft_sum, draft_out), (key_blocks, value_blocks, request_blocks, start_blocks))
    total_max, total_sum, total_out = finals
    attention = (total_out / total_sum[..., None]).astype(jnp.bfloat16)
    attention = attention.reshape(REQUESTS, KVH, DRAFT, groups, HD).transpose(0, 2, 1, 3, 4).reshape(ROWS, H * HD)
    attn_out = jnp.dot(attention, w_out, preferred_element_type=jnp.float32)
    residual = (hidden_f + attn_out).astype(jnp.bfloat16)
    residual_f = residual.astype(jnp.float32)
    post_square = lax.optimization_barrier(jnp.mean(residual_f * residual_f, axis=1, keepdims=True))
    normed = (residual_f * post_gain.astype(jnp.float32) * lax.rsqrt(post_square + EPSILON)).astype(jnp.bfloat16)
    gate_sum = jnp.dot(normed, w_gate, preferred_element_type=jnp.float32)
    up_sum = jnp.dot(normed, w_up, preferred_element_type=jnp.float32)
    hidden_mid = (jax.nn.silu(gate_sum) * up_sum).astype(jnp.bfloat16)
    next_hidden = (residual_f + jnp.dot(hidden_mid, w_down, preferred_element_type=jnp.float32)).astype(jnp.bfloat16)
    return (next_hidden, draft_keys.reshape(ROWS, KVH * HD), draft_values)
```

```python
import functools
import math

import jax
import jax.numpy as jnp
import numpy as np
from jax import lax
from jax.experimental import pallas as pl
from jax.experimental.pallas import tpu as pltpu
from jax.sharding import PartitionSpec as P

HD = 128
DRAFT = 4
BLOCK = 128
EPSILON = 1e-05
THETA_BASE = 500000.0
FLOOR = -1e30
LOG2E = math.log2(math.e)
EXP_SCALE = LOG2E / math.sqrt(HD)
UNROLL = 8
MESH = pl.DeviceIdType.MESH
F32 = jnp.float32
BF16 = jnp.bfloat16


def iota(shape, dim):
    return lax.broadcasted_iota(jnp.int32, shape, dim)


def dot(a, b):
    return jnp.dot(a, b, preferred_element_type=F32)


def dot_t(a, b):
    return lax.dot_general(a, b, (((1,), (1,)), ((), ())), preferred_element_type=F32)


def three_parts(x):
    high = x.astype(BF16).astype(F32)
    middle = (x - high).astype(BF16).astype(F32)
    return high, middle, x - high - middle


def kernel(
    nk,
    nh,
    width,
    hid_ref,
    gain_ref,
    post_ref,
    freq_ref,
    wq_hbm,
    wk_hbm,
    wv_hbm,
    wo_hbm,
    wg_hbm,
    wu_hbm,
    wd_hbm,
    keys_hbm,
    values_hbm,
    ctx_ref,
    req_ref,
    start_ref,
    next_ref,
    dkey_ref,
    dval_ref,
    wq,
    wk,
    wv,
    wo,
    wg,
    wu,
    wd,
    keys,
    values,
    hid8,
    send1,
    recv1,
    gath1,
    queries,
    scores,
    runs,
    tops,
    outs,
    sums,
    lasts,
    send2,
    recv2,
    gath2,
    send3,
    recv3,
    gath3,
    send4,
    recv4,
    gath4,
    send5,
    recv5,
    gath5,
    local_sem,
    ksend_sem,
    krecv_sem,
    hsend_sem,
    hrecv_sem,
):
    me_k = lax.axis_index("kvp")
    me_h = lax.axis_index("head")
    nm = nk // 2
    rows = 8 * nm
    me_m, me_c = me_k // 2, me_k % 2
    slots = keys.shape[0]
    db = hid_ref.shape[1]
    half = db // 2
    ff = wg.shape[1]
    fh = ff // 2
    fq = fh // 2

    first_copies = [
        pltpu.make_async_copy(src, dst, local_sem.at[i])
        for i, (src, dst) in enumerate([(wq_hbm, wq), (wk_hbm, wk), (wv_hbm, wv)])
    ]
    later_copies = [
        pltpu.make_async_copy(src, dst, local_sem.at[3 + i])
        for i, (src, dst) in enumerate(
            [(keys_hbm, keys), (values_hbm, values), (wo_hbm, wo), (wg_hbm, wg), (wu_hbm, wu), (wd_hbm, wd)]
        )
    ]
    for c in first_copies:
        c.start()

    barrier = pltpu.get_barrier_semaphore()

    def greet_k(k, _):
        pl.semaphore_signal(barrier, inc=1, device_id=(lax.rem(me_k + k, nk), me_h), device_id_type=MESH)
        return 0

    def greet_h(k, _):
        pl.semaphore_signal(barrier, inc=1, device_id=(me_k, lax.rem(me_h + k, nh)), device_id_type=MESH)
        return 0

    lax.fori_loop(1, nk, greet_k, 0)
    lax.fori_loop(1, nh, greet_h, 0)

    def kvp_copy(phase, k, src, dst):
        to = lax.rem(me_k + k, nk)
        return pltpu.make_async_remote_copy(
            src_ref=src,
            dst_ref=dst,
            send_sem=ksend_sem.at[phase, k],
            recv_sem=krecv_sem.at[phase, me_k],
            device_id=(to, me_h),
            device_id_type=MESH,
        )

    def kvp_wait(phase, source, ref):
        pltpu.make_async_remote_copy(
            src_ref=ref,
            dst_ref=ref,
            send_sem=ksend_sem.at[phase, 0],
            recv_sem=krecv_sem.at[phase, source],
            device_id=(source, me_h),
            device_id_type=MESH,
        ).wait_recv()

    def head_copy(phase, k, src, dst):
        to = lax.rem(me_h + k, nh)
        return pltpu.make_async_remote_copy(
            src_ref=src,
            dst_ref=dst,
            send_sem=hsend_sem.at[phase, k],
            recv_sem=hrecv_sem.at[phase, me_h],
            device_id=(me_k, to),
            device_id_type=MESH,
        )

    def head_wait(phase, source, ref):
        pltpu.make_async_remote_copy(
            src_ref=ref,
            dst_ref=ref,
            send_sem=hsend_sem.at[phase, 0],
            recv_sem=hrecv_sem.at[phase, source],
            device_id=(me_k, source),
            device_id_type=MESH,
        ).wait_recv()

    def kvp_scatter(phase, send, recv, only=None):
        def step(k, _):
            to = lax.rem(me_k + k, nk)
            copy = kvp_copy(phase, k, send.at[to // 2, to % 2], recv.at[me_k])
            if only is None:
                copy.start()
            else:
                pl.when(to % 2 == only)(copy.start)
            return 0

        lax.fori_loop(1, nk, step, 0)

    def kvp_gather(phase, gath):
        def step(k, _):
            kvp_copy(phase, k, gath.at[me_m, me_c], gath.at[me_m, me_c]).start()
            return 0

        lax.fori_loop(1, nk, step, 0)

    def kvp_gather_wait(phase, gath):
        def step(k, _):
            source = lax.rem(me_k + k, nk)
            kvp_wait(phase, source, gath.at[source // 2, source % 2])
            return 0

        lax.fori_loop(1, nk, step, 0)

    def kvp_reduce(phase, send, recv):
        def step(k, total):
            source = lax.rem(me_k + k, nk)
            kvp_wait(phase, source, recv.at[source])
            return total + recv[source].astype(F32)

        return lax.fori_loop(1, nk, step, send[me_m, me_c].astype(F32))

    def head_sum(phase, part, send, recv):
        parts = part.reshape(nh, 8, db)
        send[...] = jnp.concatenate([parts[:, :, :half], parts[:, :, half:]], axis=1).astype(BF16)

        def scatter(k, _):
            to = lax.rem(me_h + k, nh)
            head_copy(phase, k, send.at[to], recv.at[me_h]).start()
            return 0

        lax.fori_loop(1, nh, scatter, 0)

        def step(k, total):
            source = lax.rem(me_h + k, nh)
            head_wait(phase, source, recv.at[source])
            return total + recv[source].astype(F32)

        return lax.fori_loop(1, nh, step, send[me_h].astype(F32))

    def head_gather(phase, gath):
        def step(k, _):
            head_copy(phase, k, gath.at[me_h], gath.at[me_h]).start()
            return 0

        lax.fori_loop(1, nh, step, 0)

        def wait(k, _):
            source = lax.rem(me_h + k, nh)
            head_wait(phase, source, gath.at[source])
            return 0

        lax.fori_loop(1, nh, wait, 0)

    def folded(x):
        return jnp.concatenate([x[:, : x.shape[1] // 2], x[:, x.shape[1] // 2 :]], axis=0)

    hidden = hid_ref[...].astype(F32)
    hid8[...] = hidden.reshape(nh, 8, db)
    scaled = (hidden * gain_ref[...].astype(F32)).astype(BF16)
    square = jnp.sum(hidden * hidden, axis=1, keepdims=True)
    lane = iota((rows, HD), 1)

    def square_tile(column):
        high, middle, low = three_parts(jnp.broadcast_to(column, (rows, HD)))
        return jnp.where(lane == 0, high, jnp.where(lane == 1, middle, jnp.where(lane == 2, low, 0.0)))

    square_in = square_tile(square)
    for c in first_copies:
        c.wait()
    for c in later_copies:
        c.start()
    key_part = dot(scaled, wk[...])
    value_part = dot(scaled, wv[...])
    for c in range(2):
        query_part = dot(scaled, wq[:, c * 512 : (c + 1) * 512])
        upper = query_part[:, :384]
        lower = jnp.concatenate([query_part[:, 384:], value_part if c else key_part, square_in], axis=1)
        send1[:, c] = jnp.concatenate([upper.reshape(nm, 8, 384), lower.reshape(nm, 8, 384)], axis=1).astype(BF16)

    pl.semaphore_wait(barrier, nk + nh - 2)
    kvp_scatter(0, send1, recv1)

    eight = iota((8, HD), 0)
    lane8 = iota((8, HD), 1)
    position = jnp.where(eight < DRAFT, ctx_ref[2 * me_m], ctx_ref[2 * me_m + 1]) + eight % DRAFT
    angle = position.astype(F32) * freq_ref[...]
    cosine = jnp.cos(angle)
    sine = jnp.sin(angle)
    sine = jnp.where(lane8 < HD // 2, -sine, sine)

    def find_last(s, last):
        return jnp.where(lane8 == req_ref[s], s, last)

    lasts[...] = lax.fori_loop(0, slots, find_last, jnp.full((8, HD), -1, jnp.int32), unroll=8)

    total = kvp_reduce(0, send1, recv1)
    square_sum = jnp.sum(total[8:, 256:], axis=1, keepdims=True)
    inverse = lax.rsqrt(square_sum / width + EPSILON)
    tiles = [total[:8, :128], total[:8, 128:256], total[:8, 256:], total[8:, :128], total[8:, 128:256]]
    tiles = [t * inverse for t in tiles]
    rotated = [t * cosine + pltpu.roll(t, HD // 2, 1) * sine for t in tiles]
    low_rows = eight < DRAFT

    def swap(x):
        return pltpu.roll(x, DRAFT, 0)

    def first_of(a, b):
        return jnp.where(low_rows, a, swap(b))

    def second_of(a, b):
        return jnp.where(low_rows, swap(a), b)

    q0, q1, q2, q3 = rotated[:4]
    pair = jnp.where(me_c == 0, rotated[4], tiles[4])
    gath1[me_m, me_c, 0] = jnp.concatenate([first_of(q0, q1), first_of(q2, q3)], axis=0).astype(BF16)
    gath1[me_m, me_c, 1] = jnp.concatenate([second_of(q0, q1), second_of(q2, q3)], axis=0).astype(BF16)
    gath1[me_m, me_c, 2] = jnp.concatenate([pair, jnp.zeros_like(pair)], axis=0).astype(BF16)
    kvp_gather(1, gath1)
    kvp_gather_wait(1, gath1)
    for m in range(nm):
        for s in range(2):
            queries[2 * m + s, :16] = gath1[m, 0, s]
            queries[2 * m + s, 16:] = gath1[m, 1, s]
    drafts = [
        jnp.concatenate([gath1[m, c, 2].astype(F32)[:8] for m in range(nm)], axis=0).astype(BF16) for c in range(2)
    ]
    dkey_ref[...] = drafts[0]
    dval_ref[...] = drafts[1]

    later_copies[0].wait()
    token = iota((32, BLOCK), 1)

    def previous(s):
        return req_ref[jnp.maximum(s - 1, 0)]

    def score_step(i, run):
        for u in range(UNROLL):
            s = i * UNROLL + u
            r = req_ref[s]
            safe = jnp.maximum(r, 0)
            live = jnp.where(r >= 0, ctx_ref[safe] - start_ref[s], 0)
            part = jnp.where(token < live, dot_t(queries[safe], keys[s]), FLOOR)
            scores[s] = part
            run = jnp.maximum(part, jnp.where(r == previous(s), run, FLOOR))
            runs[s] = run
        return run

    floor_tile = jnp.full((32, BLOCK), FLOOR, F32)
    lax.fori_loop(0, slots // UNROLL, score_step, floor_tile)
    last_of = [jnp.max(jnp.where(lane8 == b, lasts[...], -1)) for b in range(nk)]
    for b in range(nk):
        run = runs[jnp.maximum(last_of[b], 0)]
        top = jnp.max(run, axis=1, keepdims=True)
        tops[b] = jnp.where(last_of[b] >= 0, jnp.broadcast_to(top, (32, BLOCK)), FLOOR)

    later_copies[1].wait()

    def value_step(i, carry):
        sum_run, out_run = carry
        for u in range(UNROLL):
            s = i * UNROLL + u
            r = req_ref[s]
            keep = jnp.where(r == previous(s), 1.0, 0.0).astype(F32)
            weight = jnp.exp2((scores[s] - tops[jnp.maximum(r, 0)]) * EXP_SCALE)
            sum_run = sum_run * keep + weight
            out_run = out_run * keep + dot(weight.astype(BF16), values[s])
            sums[s] = sum_run
            outs[s] = out_run
        return sum_run, out_run

    zero_tile = jnp.zeros((32, BLOCK), F32)
    lax.fori_loop(0, slots // UNROLL, value_step, (zero_tile, zero_tile))

    lane32 = iota((32, HD), 1)
    stats = zero_tile
    totals = []
    for b in range(nk):
        at = jnp.maximum(last_of[b], 0)
        here = last_of[b] >= 0
        out = jnp.where(here, outs[at], 0.0)
        column = jnp.sum(sums[at], axis=1, keepdims=True)
        totals.append(jnp.where(here, jnp.broadcast_to(column, (32, HD)), 0.0))
        for c in range(2):
            send2[b // 2, c, 16 * (b % 2) : 16 * (b % 2) + 16, :] = out[16 * c : 16 * c + 16].astype(BF16)
    for m in range(nm):
        for c in range(2):
            j = 2 * m + c
            part = slice(16 * c, 16 * c + 16)
            top = jnp.concatenate([tops[2 * m, part], tops[2 * m + 1, part]], axis=0)
            summed = jnp.concatenate([totals[2 * m][part], totals[2 * m + 1][part]], axis=0)
            stats = jnp.where(lane32 // 8 == j, jnp.where(lane32 % 8 < 3, top, summed), stats)
    high, middle, low = three_parts(stats)
    kind = lane32 % 8
    stats = jnp.where(
        kind % 3 == 0, high, jnp.where(kind % 3 == 1, middle, low)
    )
    stats = jnp.where(kind < 6, stats, 0.0)
    turned = jnp.concatenate([stats, jnp.zeros((HD - 32, HD), F32)], axis=0).T
    for m in range(nm):
        for c in range(2):
            j = 2 * m + c
            tile = jnp.concatenate([turned[8 * j : 8 * j + 8], jnp.zeros((8, HD), F32)], axis=0)
            send2[m, c, 32:48, :] = tile.astype(BF16)
    kvp_scatter(2, send2, recv2)

    mine = jnp.concatenate([gath1[me_m, me_c, 0], gath1[me_m, me_c, 1]], axis=0)
    draft_score = dot_t(mine, gath1[me_m, 0, 2])
    row16, col16 = iota((32, 16), 0), iota((32, 16), 1)
    seen = (col16 // DRAFT == row16 // 16) & (col16 % DRAFT <= row16 % DRAFT)
    draft_score = jnp.where(seen, draft_score, FLOOR)
    draft_top = jnp.max(draft_score, axis=1, keepdims=True)
    draft_weight = jnp.where(seen, jnp.exp2((draft_score - draft_top) * EXP_SCALE), 0.0)
    draft_sum = jnp.sum(draft_weight, axis=1, keepdims=True)
    draft_out = dot(draft_weight.astype(BF16), gath1[me_m, 1, 2])

    recv2[me_k] = send2[me_m, me_c]

    def wait2(k, _):
        source = lax.rem(me_k + k, nk)
        kvp_wait(2, source, recv2.at[source])
        return 0

    lax.fori_loop(1, nk, wait2, 0)
    every = [recv2[i, 32:48, :].astype(F32)[:8] for i in range(nk)]
    every = jnp.concatenate(every + [jnp.zeros((8, HD), F32)] * (HD // 8 - nk), axis=0)
    turned = every.T[:32]
    joined = turned + pltpu.roll(turned, HD - 1, 1) + pltpu.roll(turned, HD - 2, 1)
    own_lane = (lane32 % 8 == 0) & (lane32 < 8 * nk)
    peak = jnp.max(jnp.where(own_lane, joined, FLOOR), axis=1, keepdims=True)
    peak = jnp.maximum(peak, draft_top)
    factor = jnp.where(own_lane, jnp.exp2((joined - peak) * EXP_SCALE), 0.0)
    whole = jnp.where(own_lane, factor * pltpu.roll(joined, HD - 3, 1), 0.0)
    draft_factor = jnp.exp2((draft_top - peak) * EXP_SCALE)
    whole = jnp.sum(whole, axis=1, keepdims=True) + draft_sum * draft_factor
    factor = factor / whole
    mixed = draft_out * (draft_factor / whole)
    for i in range(nk):
        mixed = mixed + recv2[i, :32, :].astype(F32) * factor[:, 8 * i : 8 * i + 1]
    a0, a1, b0, b1 = mixed[:8], mixed[8:16], mixed[16:24], mixed[24:]
    h0, h1 = first_of(a0, b0), second_of(a0, b0)
    h2, h3 = first_of(a1, b1), second_of(a1, b1)
    gath2[me_m, me_c] = jnp.concatenate(
        [jnp.concatenate([h0, h1], axis=1), jnp.concatenate([h2, h3], axis=1)], axis=0
    ).astype(BF16)
    kvp_gather(3, gath2)
    later_copies[2].wait()
    kvp_gather_wait(3, gath2)

    attn_part = jnp.zeros((rows, db), F32)
    for c in range(2):
        for g in range(2):
            piece = jnp.concatenate(
                [gath2[m, c].astype(F32)[8 * g : 8 * g + 8] for m in range(nm)], axis=0
            ).astype(BF16)
            attn_part += dot(piece, wo[512 * c + 256 * g : 512 * c + 256 * g + 256, :])
    attn = head_sum(0, attn_part, send3, recv3)
    gath3[me_h] = (folded(hid8[me_h]) + attn).astype(BF16)
    head_gather(1, gath3)

    def unfolded(gath):
        pieces = [gath[h].astype(F32) for h in range(nh)]
        return jnp.concatenate(
            [jnp.concatenate([p[:8] for p in pieces], axis=0), jnp.concatenate([p[8:] for p in pieces], axis=0)],
            axis=1,
        )

    residual = unfolded(gath3)
    square_out = square_tile(jnp.sum(residual * residual, axis=1, keepdims=True)).reshape(nm, 8, HD)
    normed = (residual * post_ref[...].astype(F32)).astype(BF16)
    chunk = 256 if fh % 256 == 0 else 128
    later_copies[3].wait()
    later_copies[4].wait()
    for c in range(2):

        def up_step(i, _):
            at = pl.multiple_of(c * fh + i * chunk, chunk)
            gate = dot(normed, wg[:, pl.ds(at, chunk)]).reshape(nm, 8, chunk)
            up = dot(normed, wu[:, pl.ds(at, chunk)]).reshape(nm, 8, chunk)
            send4[:, c, :, pl.ds(pl.multiple_of(i * chunk, chunk), chunk)] = jnp.concatenate(
                [gate, up], axis=1
            ).astype(BF16)
            return 0

        lax.fori_loop(0, fh // chunk, up_step, 0)
        send4[:, c, :, fh:] = jnp.concatenate([square_out, jnp.zeros_like(square_out)], axis=1).astype(BF16)
        kvp_scatter(4, send4, recv4, only=c)
    total = kvp_reduce(4, send4, recv4)
    square_sum = jnp.sum(total[:8, fh:], axis=1, keepdims=True)
    inverse = lax.rsqrt(square_sum / width + EPSILON)
    gate = total[:8, :fh] * inverse
    up = total[8:, :fh] * inverse
    middle = gate / (1.0 + jnp.exp(-gate)) * up
    gath4[me_m, me_c] = folded(middle).astype(BF16)
    kvp_gather(5, gath4)
    later_copies[5].wait()
    kvp_gather_wait(5, gath4)
    down_part = jnp.zeros((rows, db), F32)
    for c in range(2):
        for g in range(2):
            piece = jnp.concatenate(
                [gath4[m, c].astype(F32)[8 * g : 8 * g + 8] for m in range(nm)], axis=0
            ).astype(BF16)
            at = fh * c + fq * g
            down_part += dot(piece, wd[at : at + fq, :])
    down = head_sum(2, down_part, send5, recv5)
    gath5[me_h] = (gath3[me_h].astype(F32) + down).astype(BF16)
    head_gather(3, gath5)
    next_ref[...] = unfolded(gath5).astype(BF16)

    def kvp_done(k, _):
        for phase, ref in ((0, recv1), (2, recv2), (4, recv4)):
            kvp_copy(phase, k, ref.at[0], ref.at[0]).wait_send()
        for phase, ref in ((1, gath1), (3, gath2), (5, gath4)):
            kvp_copy(phase, k, ref.at[0, 0], ref.at[0, 0]).wait_send()
        return 0

    lax.fori_loop(1, nk, kvp_done, 0)

    def head_done(k, _):
        for phase, ref in ((0, recv3), (1, gath3), (2, recv5), (3, gath5)):
            head_copy(phase, k, ref.at[0], ref.at[0]).wait_send()
        return 0

    lax.fori_loop(1, nh, head_done, 0)


def body(
    nk,
    nh,
    hidden_in,
    norm_gain,
    w_query,
    w_key,
    w_value,
    w_out,
    post_gain,
    w_gate,
    w_up,
    w_down,
    cache_keys,
    cache_values,
    context_len,
    slot_request,
    slot_start,
):
    rows, db = hidden_in.shape
    nm = nk // 2
    slots = cache_keys.shape[0]
    fh = w_gate.shape[1] // 2
    exponent = np.arange(HD // 2, dtype=np.float32) * np.float32(2.0 / HD)
    frequency = (THETA_BASE ** (-exponent.astype(np.float64))).astype(np.float32)
    frequency = jnp.asarray(np.concatenate([frequency, frequency])[None, :])
    vmem = pl.BlockSpec(memory_space=pltpu.VMEM)
    hbm = pl.BlockSpec(memory_space=pl.ANY)
    smem = pl.BlockSpec(memory_space=pltpu.SMEM)
    scratch = [
        pltpu.VMEM(w.shape, BF16)
        for w in (w_query, w_key, w_value, w_out, w_gate, w_up, w_down, cache_keys, cache_values)
    ]
    scratch += [
        pltpu.VMEM((nh, 8, db), F32),
        pltpu.VMEM((nm, 2, 16, 384), BF16),
        pltpu.VMEM((nk, 16, 384), BF16),
        pltpu.VMEM((nm, 2, 3, 16, HD), BF16),
        pltpu.VMEM((nk, 32, HD), BF16),
        pltpu.VMEM((slots, 32, BLOCK), F32),
        pltpu.VMEM((slots, 32, BLOCK), F32),
        pltpu.VMEM((nk, 32, BLOCK), F32),
        pltpu.VMEM((slots, 32, HD), F32),
        pltpu.VMEM((slots, 32, BLOCK), F32),
        pltpu.VMEM((8, HD), jnp.int32),
        pltpu.VMEM((nm, 2, 48, HD), BF16),
        pltpu.VMEM((nk, 48, HD), BF16),
        pltpu.VMEM((nm, 2, 16, 256), BF16),
        pltpu.VMEM((nh, 16, db // 2), BF16),
        pltpu.VMEM((nh, 16, db // 2), BF16),
        pltpu.VMEM((nh, 16, db // 2), BF16),
        pltpu.VMEM((nm, 2, 16, fh + HD), BF16),
        pltpu.VMEM((nk, 16, fh + HD), BF16),
        pltpu.VMEM((nm, 2, 16, fh // 2), BF16),
        pltpu.VMEM((nh, 16, db // 2), BF16),
        pltpu.VMEM((nh, 16, db // 2), BF16),
        pltpu.VMEM((nh, 16, db // 2), BF16),
        pltpu.SemaphoreType.DMA((9,)),
        pltpu.SemaphoreType.DMA((6, nk)),
        pltpu.SemaphoreType.DMA((6, nk)),
        pltpu.SemaphoreType.DMA((4, nh)),
        pltpu.SemaphoreType.DMA((4, nh)),
    ]
    weight_items = sum(w.size for w in (w_query, w_key, w_value, w_out, w_gate, w_up, w_down))
    return pl.pallas_call(
        functools.partial(kernel, nk, nh, db * nk),
        out_shape=(
            jax.ShapeDtypeStruct((rows, db), BF16),
            jax.ShapeDtypeStruct((rows, HD), BF16),
            jax.ShapeDtypeStruct((rows, HD), BF16),
        ),
        in_specs=[vmem] * 4 + [hbm] * 9 + [smem] * 3,
        out_specs=(vmem, vmem, vmem),
        scratch_shapes=scratch,
        compiler_params=pltpu.CompilerParams(
            collective_id=0, has_side_effects=True, vmem_limit_bytes=56 * 1024 * 1024
        ),
        cost_estimate=pl.CostEstimate(
            flops=2 * rows * weight_items + 4 * slots * 32 * BLOCK * HD,
            bytes_accessed=2 * (weight_items + 2 * cache_keys.size),
            transcendentals=slots * 32 * BLOCK,
        ),
    )(
        hidden_in,
        norm_gain.reshape(1, db),
        post_gain.reshape(1, db),
        frequency,
        w_query,
        w_key,
        w_value,
        w_out,
        w_gate,
        w_up,
        w_down,
        cache_keys,
        cache_values,
        context_len,
        slot_request,
        slot_start,
    )


def solution(mesh):
    return jax.shard_map(
        functools.partial(body, mesh.shape["kvp"], mesh.shape["head"]),
        mesh=mesh,
        in_specs=(
            P(None, "kvp"),
            P("kvp"),
            P("kvp", "head"),
            P("kvp", "head"),
            P("kvp", "head"),
            P("head", "kvp"),
            P("kvp"),
            P("kvp", "head"),
            P("kvp", "head"),
            P("head", "kvp"),
            P("kvp", None, "head"),
            P("kvp", None, "head"),
            P(),
            P("kvp"),
            P("kvp"),
        ),
        out_specs=(P(None, "kvp"), P(None, "head"), P(None, "head")),
        check_vma=False,
    )
```

```python
import functools
import math

import jax
import jax.numpy as jnp
import numpy as np
from jax import lax
from jax.experimental import pallas as pl
from jax.experimental.pallas import tpu as pltpu
from jax.sharding import PartitionSpec as P

HD = 128
DRAFT = 4
BLOCK = 128
EPSILON = 1e-05
THETA_BASE = 500000.0
FLOOR = -1e30
LOG2E = math.log2(math.e)
EXP_SCALE = LOG2E / math.sqrt(HD)
UNROLL = 32
MESH = pl.DeviceIdType.MESH
F32 = jnp.float32
BF16 = jnp.bfloat16


def iota(shape, dim):
    return lax.broadcasted_iota(jnp.int32, shape, dim)


def dot(a, b):
    return jnp.dot(a, b, preferred_element_type=F32)


def dot_t(a, b):
    return lax.dot_general(a, b, (((1,), (1,)), ((), ())), preferred_element_type=F32)


def three_parts(x):
    high = x.astype(BF16).astype(F32)
    middle = (x - high).astype(BF16).astype(F32)
    return high, middle, x - high - middle


def pieces_of(columns):
    size = 512 if columns > 512 else columns // 2
    return [(at, min(size, columns - at)) for at in range(0, columns, size)]


def hand_on(*refs):
    sources, targets, sem = refs[:3], refs[3:6], refs[6]
    copies = [pltpu.make_async_copy(a, b, sem.at[i]) for i, (a, b) in enumerate(zip(sources, targets))]
    for copy in copies:
        copy.start()
    for copy in copies:
        copy.wait()


def kernel(
    nk,
    nh,
    width,
    hid_ref,
    gain_ref,
    post_ref,
    freq_ref,
    wq_hbm,
    wk_hbm,
    wv_hbm,
    wo_hbm,
    wg_hbm,
    wu_hbm,
    wd_hbm,
    keys_hbm,
    values_hbm,
    ctx_ref,
    req_ref,
    start_ref,
    next_ref,
    dkey_ref,
    dval_ref,
    wq,
    wk,
    wv,
    wo,
    wg,
    wu,
    wd,
    keys,
    values,
    hidden_halves,
    send1,
    recv1,
    gath1,
    queries,
    scores,
    runs,
    tops,
    outs,
    sums,
    lasts,
    send2,
    recv2,
    gath2,
    core3,
    along3,
    resid,
    send_sq,
    recv_sq,
    send4,
    recv4,
    gath4,
    core5,
    along5,
    final,
    local_sem,
    ksend_sem,
    krecv_sem,
    hsend_sem,
    hrecv_sem,
):
    me_k = lax.axis_index("kvp")
    me_h = lax.axis_index("head")
    nm = nk // 2
    nz = nh // 2
    me_z, core = me_h // 2, me_h % 2
    twin = me_h + 1 - 2 * core

    def along_z(k):
        return lax.rem(me_z + k, nz) * 2 + core

    rows = 8 * nm
    me_m, me_c = me_k // 2, me_k % 2
    slots = keys.shape[0]
    db = hid_ref.shape[1]
    half = db // 2
    ff = wg.shape[1]
    fh = ff // 2
    pieces = pieces_of(fh)

    started = []
    sent = []

    first_copies = [
        pltpu.make_async_copy(src, dst, local_sem.at[i])
        for i, (src, dst) in enumerate([(wq_hbm, wq), (wk_hbm, wk), (wv_hbm, wv)])
    ]
    later_copies = [
        pltpu.make_async_copy(src, dst, local_sem.at[3 + i])
        for i, (src, dst) in enumerate(
            [(keys_hbm, keys), (values_hbm, values), (wo_hbm, wo), (wg_hbm, wg), (wu_hbm, wu), (wd_hbm, wd)]
        )
    ]
    def arrive(i):
        later_copies[i].wait()

    for c in first_copies:
        c.start()

    barrier = pltpu.get_barrier_semaphore()

    def greet_k(k, _):
        pl.semaphore_signal(barrier, inc=1, device_id=(lax.rem(me_k + k, nk), me_h), device_id_type=MESH)
        return 0

    lax.fori_loop(1, nk, greet_k, 0)
    for to in [twin] + [along_z(k) for k in range(1, nz)]:
        pl.semaphore_signal(barrier, inc=1, device_id=(me_k, to), device_id_type=MESH)

    def kvp_copy(phase, k, src, dst):
        to = lax.rem(me_k + k, nk)
        return pltpu.make_async_remote_copy(
            src_ref=src,
            dst_ref=dst,
            send_sem=ksend_sem.at[phase, k],
            recv_sem=krecv_sem.at[phase, me_k],
            device_id=(to, me_h),
            device_id_type=MESH,
        )

    def kvp_wait(phase, source, ref):
        pltpu.make_async_remote_copy(
            src_ref=ref,
            dst_ref=ref,
            send_sem=ksend_sem.at[phase, 0],
            recv_sem=krecv_sem.at[phase, source],
            device_id=(source, me_h),
            device_id_type=MESH,
        ).wait_recv()

    def head_copy(sem, to, src, dst):
        return pltpu.make_async_remote_copy(
            src_ref=src,
            dst_ref=dst,
            send_sem=hsend_sem.at[sem],
            recv_sem=hrecv_sem.at[sem],
            device_id=(me_k, to),
            device_id_type=MESH,
        )

    def kvp_scatter(phase, send, recv):
        started.append((kvp_copy, phase, recv.at[0], range(1, nk)))

        def step(k, _):
            to = lax.rem(me_k + k, nk)
            kvp_copy(phase, k, send.at[to // 2, to % 2], recv.at[me_k]).start()
            return 0

        lax.fori_loop(1, nk, step, 0)

    def kvp_gather(phase, gath):
        mine = gath.at[me_m, me_c]
        started.append((kvp_copy, phase, mine, range(1, nk)))

        def step(k, _):
            kvp_copy(phase, k, mine, mine).start()
            return 0

        lax.fori_loop(1, nk, step, 0)

    def kvp_gather_wait(phase, gath):
        def step(k, _):
            source = lax.rem(me_k + k, nk)
            kvp_wait(phase, source, gath.at[source // 2, source % 2])
            return 0

        lax.fori_loop(1, nk, step, 0)

    def kvp_reduce(phase, send, recv):
        def step(k, total):
            source = lax.rem(me_k + k, nk)
            kvp_wait(phase, source, recv.at[source])
            return total + recv[source].astype(F32)

        return lax.fori_loop(1, nk, step, send[me_m, me_c].astype(F32))

    def halves(x):
        return x[:, :half], x[:, half:]

    def own_half(x):
        left, right = halves(x)
        return jnp.where(core == 0, left, right), jnp.where(core == 0, right, left)

    def head_sum(base, part, swap_ref, along_ref):
        own, other = own_half(part)
        swap_ref[0] = other.astype(BF16)
        swapped = head_copy(base, twin, swap_ref.at[0], swap_ref.at[1])
        swapped.start()
        sent.append(swapped)
        swapped.wait_recv()
        along_ref[0] = (own + swap_ref[1].astype(F32)).astype(BF16)
        copies = [head_copy(base + k, along_z(k), along_ref.at[0], along_ref.at[k]) for k in range(1, nz)]
        for copy in copies:
            copy.start()
        sent.extend(copies)
        for copy in copies:
            copy.wait_recv()
        total = jnp.zeros((rows, half), F32)
        for z in range(nz):
            total = total + along_ref[lax.rem(me_z - z + nz, nz)].astype(F32)
        return total

    def share_half(sem, ref):
        copy = head_copy(sem, twin, ref.at[core], ref.at[core])
        copy.start()
        sent.append(copy)
        copy.wait_recv()

    def finish():
        for copy in sent:
            copy.wait_send()
        for copy, phase, ref, keys_of in started:

            def done(k, _, copy=copy, phase=phase, ref=ref):
                copy(phase, k, ref, ref).wait_send()
                return 0

            lax.fori_loop(keys_of.start, keys_of.stop, done, 0)

    def folded(x):
        return jnp.concatenate([x[:, : x.shape[1] // 2], x[:, x.shape[1] // 2 :]], axis=0)

    hidden = hid_ref[...].astype(F32)
    hidden_halves[0], hidden_halves[1] = halves(hidden)
    scaled = (hidden * gain_ref[...].astype(F32).reshape(1, db)).astype(BF16)
    square = jnp.sum(hidden * hidden, axis=1, keepdims=True)
    lane = iota((rows, HD), 1)

    def square_tile(column):
        high, middle, low = three_parts(jnp.broadcast_to(column, (rows, HD)))
        return jnp.where(lane == 0, high, jnp.where(lane == 1, middle, jnp.where(lane == 2, low, 0.0)))

    square_in = square_tile(square)
    for c in first_copies:
        c.wait()
    for c in later_copies:
        c.start()
    key_part = dot(scaled, wk[...])
    value_part = dot(scaled, wv[...])
    for c in range(2):
        query_part = dot(scaled, wq[:, c * 512 : (c + 1) * 512])
        upper = query_part[:, :384]
        lower = jnp.concatenate([query_part[:, 384:], value_part if c else key_part, square_in], axis=1)
        send1[:, c] = jnp.concatenate([upper.reshape(nm, 8, 384), lower.reshape(nm, 8, 384)], axis=1).astype(BF16)

    pl.semaphore_wait(barrier, nk + nz - 1)
    kvp_scatter(0, send1, recv1)

    eight = iota((8, HD), 0)
    lane8 = iota((8, HD), 1)
    position = jnp.where(eight < DRAFT, ctx_ref[2 * me_m], ctx_ref[2 * me_m + 1]) + eight % DRAFT
    angle = position.astype(F32) * freq_ref[...]
    cosine = jnp.cos(angle)
    sine = jnp.sin(angle)
    sine = jnp.where(lane8 < HD // 2, -sine, sine)

    def find_last(s, last):
        return jnp.where(lane8 == req_ref[s], s, last)

    lasts[...] = lax.fori_loop(0, slots, find_last, jnp.full((8, HD), -1, jnp.int32), unroll=8)

    total = kvp_reduce(0, send1, recv1)
    square_sum = jnp.sum(total[8:, 256:], axis=1, keepdims=True)
    inverse = lax.rsqrt(square_sum / width + EPSILON)
    tiles = [total[:8, :128], total[:8, 128:256], total[:8, 256:], total[8:, :128], total[8:, 128:256]]
    tiles = [t * inverse for t in tiles]
    rotated = [t * cosine + pltpu.roll(t, HD // 2, 1) * sine for t in tiles]
    low_rows = eight < DRAFT

    def swap(x):
        return pltpu.roll(x, DRAFT, 0)

    def first_of(a, b):
        return jnp.where(low_rows, a, swap(b))

    def second_of(a, b):
        return jnp.where(low_rows, swap(a), b)

    q0, q1, q2, q3 = rotated[:4]
    pair = jnp.where(me_c == 0, rotated[4], tiles[4])
    gath1[me_m, me_c, 0] = jnp.concatenate([first_of(q0, q1), first_of(q2, q3)], axis=0).astype(BF16)
    gath1[me_m, me_c, 1] = jnp.concatenate([second_of(q0, q1), second_of(q2, q3)], axis=0).astype(BF16)
    gath1[me_m, me_c, 2] = jnp.concatenate([pair, jnp.zeros_like(pair)], axis=0).astype(BF16)
    kvp_gather(1, gath1)
    kvp_gather_wait(1, gath1)
    for m in range(nm):
        for s in range(2):
            queries[2 * m + s, :16] = gath1[m, 0, s]
            queries[2 * m + s, 16:] = gath1[m, 1, s]
    drafts = [
        jnp.concatenate([gath1[m, c, 2].astype(F32)[:8] for m in range(nm)], axis=0).astype(BF16) for c in range(2)
    ]
    dkey_ref[...] = drafts[0]
    dval_ref[...] = drafts[1]

    arrive(0)
    token = iota((32, BLOCK), 1)

    def previous(s):
        return req_ref[jnp.maximum(s - 1, 0)]

    def score_step(i, run):
        for u in range(UNROLL):
            s = i * UNROLL + u
            r = req_ref[s]
            safe = jnp.maximum(r, 0)
            live = jnp.where(r >= 0, ctx_ref[safe] - start_ref[s], 0)
            part = jnp.where(token < live, dot_t(queries[safe], keys[s]), FLOOR)
            scores[s] = part
            run = jnp.maximum(part, jnp.where(r == previous(s), run, FLOOR))
            runs[s] = run
        return run

    floor_tile = jnp.full((32, BLOCK), FLOOR, F32)
    lax.fori_loop(0, slots // UNROLL, score_step, floor_tile)
    last_of = [jnp.max(jnp.where(lane8 == b, lasts[...], -1)) for b in range(nk)]
    for b in range(nk):
        run = runs[jnp.maximum(last_of[b], 0)]
        top = jnp.max(run, axis=1, keepdims=True)
        tops[b] = jnp.where(last_of[b] >= 0, jnp.broadcast_to(top, (32, BLOCK)), FLOOR)

    arrive(1)

    def value_step(i, carry):
        sum_run, out_run = carry
        for u in range(UNROLL):
            s = i * UNROLL + u
            r = req_ref[s]
            keep = jnp.where(r == previous(s), 1.0, 0.0).astype(F32)
            weight = jnp.exp2((scores[s] - tops[jnp.maximum(r, 0)]) * EXP_SCALE)
            sum_run = sum_run * keep + weight
            out_run = out_run * keep + dot(weight.astype(BF16), values[s])
            sums[s] = sum_run
            outs[s] = out_run
        return sum_run, out_run

    zero_tile = jnp.zeros((32, BLOCK), F32)
    lax.fori_loop(0, slots // UNROLL, value_step, (zero_tile, zero_tile))

    lane32 = iota((32, HD), 1)
    stats = zero_tile
    totals = []
    for b in range(nk):
        at = jnp.maximum(last_of[b], 0)
        here = last_of[b] >= 0
        out = jnp.where(here, outs[at], 0.0)
        column = jnp.sum(sums[at], axis=1, keepdims=True)
        totals.append(jnp.where(here, jnp.broadcast_to(column, (32, HD)), 0.0))
        for c in range(2):
            send2[b // 2, c, 16 * (b % 2) : 16 * (b % 2) + 16, :] = out[16 * c : 16 * c + 16].astype(BF16)
    for m in range(nm):
        for c in range(2):
            j = 2 * m + c
            part = slice(16 * c, 16 * c + 16)
            top = jnp.concatenate([tops[2 * m, part], tops[2 * m + 1, part]], axis=0)
            summed = jnp.concatenate([totals[2 * m][part], totals[2 * m + 1][part]], axis=0)
            stats = jnp.where(lane32 // 8 == j, jnp.where(lane32 % 8 < 3, top, summed), stats)
    high, middle, low = three_parts(stats)
    kind = lane32 % 8
    stats = jnp.where(
        kind % 3 == 0, high, jnp.where(kind % 3 == 1, middle, low)
    )
    stats = jnp.where(kind < 6, stats, 0.0)
    turned = jnp.concatenate([stats, jnp.zeros((HD - 32, HD), F32)], axis=0).T
    for m in range(nm):
        for c in range(2):
            j = 2 * m + c
            tile = jnp.concatenate([turned[8 * j : 8 * j + 8], jnp.zeros((8, HD), F32)], axis=0)
            send2[m, c, 32:48, :] = tile.astype(BF16)
    kvp_scatter(2, send2, recv2)

    mine = jnp.concatenate([gath1[me_m, me_c, 0], gath1[me_m, me_c, 1]], axis=0)
    draft_score = dot_t(mine, gath1[me_m, 0, 2])
    row16, col16 = iota((32, 16), 0), iota((32, 16), 1)
    seen = (col16 // DRAFT == row16 // 16) & (col16 % DRAFT <= row16 % DRAFT)
    draft_score = jnp.where(seen, draft_score, FLOOR)
    draft_top = jnp.max(draft_score, axis=1, keepdims=True)
    draft_weight = jnp.where(seen, jnp.exp2((draft_score - draft_top) * EXP_SCALE), 0.0)
    draft_sum = jnp.sum(draft_weight, axis=1, keepdims=True)
    draft_out = dot(draft_weight.astype(BF16), gath1[me_m, 1, 2])

    recv2[me_k] = send2[me_m, me_c]

    def wait2(k, _):
        source = lax.rem(me_k + k, nk)
        kvp_wait(2, source, recv2.at[source])
        return 0

    lax.fori_loop(1, nk, wait2, 0)
    every = [recv2[i, 32:48, :].astype(F32)[:8] for i in range(nk)]
    every = jnp.concatenate(every + [jnp.zeros((8, HD), F32)] * (HD // 8 - nk), axis=0)
    turned = every.T[:32]
    joined = turned + pltpu.roll(turned, HD - 1, 1) + pltpu.roll(turned, HD - 2, 1)
    own_lane = (lane32 % 8 == 0) & (lane32 < 8 * nk)
    peak = jnp.max(jnp.where(own_lane, joined, FLOOR), axis=1, keepdims=True)
    peak = jnp.maximum(peak, draft_top)
    factor = jnp.where(own_lane, jnp.exp2((joined - peak) * EXP_SCALE), 0.0)
    whole = jnp.where(own_lane, factor * pltpu.roll(joined, HD - 3, 1), 0.0)
    draft_factor = jnp.exp2((draft_top - peak) * EXP_SCALE)
    whole = jnp.sum(whole, axis=1, keepdims=True) + draft_sum * draft_factor
    factor = factor / whole
    mixed = draft_out * (draft_factor / whole)
    for i in range(nk):
        mixed = mixed + recv2[i, :32, :].astype(F32) * factor[:, 8 * i : 8 * i + 1]
    a0, a1, b0, b1 = mixed[:8], mixed[8:16], mixed[16:24], mixed[24:]
    h0, h1 = first_of(a0, b0), second_of(a0, b0)
    h2, h3 = first_of(a1, b1), second_of(a1, b1)
    gath2[me_m, me_c] = jnp.concatenate(
        [jnp.concatenate([h0, h1], axis=1), jnp.concatenate([h2, h3], axis=1)], axis=0
    ).astype(BF16)
    kvp_gather(3, gath2)
    arrive(2)
    kvp_gather_wait(3, gath2)

    attn_part = jnp.zeros((rows, db), F32)
    for c in range(2):
        for g in range(2):
            piece = jnp.concatenate(
                [gath2[m, c].astype(F32)[8 * g : 8 * g + 8] for m in range(nm)], axis=0
            ).astype(BF16)
            attn_part += dot(piece, wo[512 * c + 256 * g : 512 * c + 256 * g + 256, :])
    attn = head_sum(0, attn_part, core3, along3)
    resid[core] = (hidden_halves[core] + attn).astype(BF16)
    share_half(nz, resid)
    residual = jnp.concatenate([resid[0].astype(F32), resid[1].astype(F32)], axis=1)
    square_out = square_tile(jnp.sum(residual * residual, axis=1, keepdims=True)).reshape(nm, 8, HD)
    square_out = jnp.concatenate([square_out, jnp.zeros_like(square_out)], axis=1).astype(BF16)
    send_sq[:, 0] = square_out
    send_sq[:, 1] = square_out
    kvp_scatter(4, send_sq, recv_sq)
    normed = (residual * post_ref[...].astype(F32).reshape(1, db)).astype(BF16)
    arrive(3)
    arrive(4)
    for p, (at, size) in enumerate(pieces):
        part = pl.ds(at, size)
        started.append((kvp_copy, 5 + p, recv4.at[0, :, part], range(1, nk)))
        for c in range(2):
            columns = slice(c * fh + at, c * fh + at + size)
            gate = dot(normed, wg[:, columns]).reshape(nm, 8, size)
            up = dot(normed, wu[:, columns]).reshape(nm, 8, size)
            send4[:, c, :, part] = jnp.concatenate([gate, up], axis=1).astype(BF16)

            def step(i, _, p=p, c=c, part=part):
                to_m = lax.rem(me_m + i, nm)
                to = 2 * to_m + c
                k = lax.rem(to - me_k + nk, nk)

                @pl.when(k != 0)
                def _():
                    kvp_copy(5 + p, k, send4.at[to_m, c, :, part], recv4.at[me_k, :, part]).start()

                return 0

            lax.fori_loop(0, nm, step, 0)
    total = kvp_reduce(4, send_sq, recv_sq)
    inverse = lax.rsqrt(jnp.sum(total[:8], axis=1, keepdims=True) / width + EPSILON)
    base = 5 + len(pieces)
    for p, (at, size) in enumerate(pieces):
        part = pl.ds(at, size)

        def add(k, total, p=p, part=part):
            source = lax.rem(me_k + k, nk)
            kvp_wait(5 + p, source, recv4.at[source, :, part])
            return total + recv4[source, :, part].astype(F32)

        total = lax.fori_loop(1, nk, add, send4[me_m, me_c, :, part].astype(F32))
        gate = total[:8] * inverse
        up = total[8:] * inverse
        middle = gate / (1.0 + jnp.exp(-gate)) * up
        mine = gath4.at[me_m, me_c, :, pl.ds(at // 2, size // 2)]
        mine[...] = folded(middle).astype(BF16)
        started.append((kvp_copy, base + p, mine, range(1, nk)))

        def share(k, _, p=p, mine=mine):
            kvp_copy(base + p, k, mine, mine).start()
            return 0

        lax.fori_loop(1, nk, share, 0)
    arrive(5)
    down_part = jnp.zeros((rows, db), F32)
    for p, (at, size) in enumerate(pieces):
        part = pl.ds(at // 2, size // 2)

        def await_hidden(k, _, p=p, part=part):
            source = lax.rem(me_k + k, nk)
            kvp_wait(base + p, source, gath4.at[source // 2, source % 2, :, part])
            return 0

        lax.fori_loop(1, nk, await_hidden, 0)
        for c in range(2):
            rows_of = [gath4[m, c, :, part].astype(F32) for m in range(nm)]
            piece = jnp.concatenate(
                [jnp.concatenate([r[:8] for r in rows_of], axis=0), jnp.concatenate([r[8:] for r in rows_of], axis=0)],
                axis=1,
            ).astype(BF16)
            down_part += dot(piece, wd[c * fh + at : c * fh + at + size, :])
    down = head_sum(nz + 1, down_part, core5, along5)
    final[core] = (resid[core].astype(F32) + down).astype(BF16)
    share_half(2 * nz + 1, final)
    next_ref[:, :half] = final[0]
    next_ref[:, half:] = final[1]
    finish()


def body(
    nk,
    nh,
    hidden_in,
    norm_gain,
    w_query,
    w_key,
    w_value,
    w_out,
    post_gain,
    w_gate,
    w_up,
    w_down,
    cache_keys,
    cache_values,
    context_len,
    slot_request,
    slot_start,
):
    rows, db = hidden_in.shape
    nm = nk // 2
    slots = cache_keys.shape[0]
    fh = w_gate.shape[1] // 2
    half, nz, count = db // 2, nh // 2, len(pieces_of(fh))
    exponent = np.arange(HD // 2, dtype=np.float32) * np.float32(2.0 / HD)
    frequency = (THETA_BASE ** (-exponent.astype(np.float64))).astype(np.float32)
    frequency = jnp.asarray(np.concatenate([frequency, frequency])[None, :])
    vmem = pl.BlockSpec(memory_space=pltpu.VMEM)
    hbm = pl.BlockSpec(memory_space=pl.ANY)
    smem = pl.BlockSpec(memory_space=pltpu.SMEM)
    scratch = [
        pltpu.VMEM(w.shape, BF16)
        for w in (w_query, w_key, w_value, w_out, w_gate, w_up, w_down, cache_keys, cache_values)
    ]
    scratch += [
        pltpu.VMEM((2, rows, half), F32),
        pltpu.VMEM((nm, 2, 16, 384), BF16),
        pltpu.VMEM((nk, 16, 384), BF16),
        pltpu.VMEM((nm, 2, 3, 16, HD), BF16),
        pltpu.VMEM((nk, 32, HD), BF16),
        pltpu.VMEM((slots, 32, BLOCK), F32),
        pltpu.VMEM((slots, 32, BLOCK), F32),
        pltpu.VMEM((nk, 32, BLOCK), F32),
        pltpu.VMEM((slots, 32, HD), F32),
        pltpu.VMEM((slots, 32, BLOCK), F32),
        pltpu.VMEM((8, HD), jnp.int32),
        pltpu.VMEM((nm, 2, 48, HD), BF16),
        pltpu.VMEM((nk, 48, HD), BF16),
        pltpu.VMEM((nm, 2, 16, 256), BF16),
        pltpu.VMEM((2, rows, half), BF16),
        pltpu.VMEM((nz, rows, half), BF16),
        pltpu.VMEM((2, rows, half), BF16),
        pltpu.VMEM((nm, 2, 16, HD), BF16),
        pltpu.VMEM((nk, 16, HD), BF16),
        pltpu.VMEM((nm, 2, 16, fh), BF16),
        pltpu.VMEM((nk, 16, fh), BF16),
        pltpu.VMEM((nm, 2, 16, fh // 2), BF16),
        pltpu.VMEM((2, rows, half), BF16),
        pltpu.VMEM((nz, rows, half), BF16),
        pltpu.VMEM((2, rows, half), BF16),
        pltpu.SemaphoreType.DMA((9,)),
        pltpu.SemaphoreType.DMA((5 + 2 * count, nk)),
        pltpu.SemaphoreType.DMA((5 + 2 * count, nk)),
        pltpu.SemaphoreType.DMA((2 * nz + 2,)),
        pltpu.SemaphoreType.DMA((2 * nz + 2,)),
    ]
    weight_items = sum(w.size for w in (w_query, w_key, w_value, w_out, w_gate, w_up, w_down))
    results = pl.pallas_call(
        functools.partial(kernel, nk, nh, db * nk),
        out_shape=(
            jax.ShapeDtypeStruct((rows, db), BF16),
            jax.ShapeDtypeStruct((rows, HD), BF16),
            jax.ShapeDtypeStruct((rows, HD), BF16),
        ),
        in_specs=[vmem] * 4 + [hbm] * 9 + [smem] * 3,
        out_specs=(vmem, vmem, vmem),
        scratch_shapes=scratch,
        compiler_params=pltpu.CompilerParams(
            collective_id=0, has_side_effects=True, vmem_limit_bytes=56 * 1024 * 1024
        ),
        cost_estimate=pl.CostEstimate(
            flops=2 * rows * weight_items + 4 * slots * 32 * BLOCK * HD,
            bytes_accessed=2 * (weight_items + 2 * cache_keys.size),
            transcendentals=slots * 32 * BLOCK,
        ),
    )(
        hidden_in,
        norm_gain,
        post_gain,
        frequency,
        w_query,
        w_key,
        w_value,
        w_out,
        w_gate,
        w_up,
        w_down,
        cache_keys,
        cache_values,
        context_len,
        slot_request,
        slot_start,
    )
    return pl.pallas_call(
        hand_on,
        out_shape=tuple(jax.ShapeDtypeStruct(r.shape, r.dtype) for r in results),
        in_specs=[hbm] * 3,
        out_specs=(hbm,) * 3,
        scratch_shapes=[pltpu.SemaphoreType.DMA((3,))],
    )(*results)


def solution(mesh):
    return jax.shard_map(
        functools.partial(body, mesh.shape["kvp"], mesh.shape["head"]),
        mesh=mesh,
        in_specs=(
            P(None, "kvp"),
            P("kvp"),
            P("kvp", "head"),
            P("kvp", "head"),
            P("kvp", "head"),
            P("head", "kvp"),
            P("kvp"),
            P("kvp", "head"),
            P("kvp", "head"),
            P("head", "kvp"),
            P("kvp", None, "head"),
            P("kvp", None, "head"),
            P(),
            P("kvp"),
            P("kvp"),
        ),
        out_specs=(P(None, "kvp"), P(None, "head"), P(None, "head")),
        check_vma=False,
    )
```

```python
import functools
import math

import jax
import jax.numpy as jnp
import numpy as np
from jax import lax
from jax.experimental import pallas as pl
from jax.experimental.pallas import tpu as pltpu
from jax.sharding import PartitionSpec as P

HD = 128
DRAFT = 4
BLOCK = 128
EPSILON = 1e-05
THETA_BASE = 500000.0
FLOOR = -1e30
LOG2E = math.log2(math.e)
EXP_SCALE = LOG2E / math.sqrt(HD)
UNROLL = 32
MESH = pl.DeviceIdType.MESH
F32 = jnp.float32
BF16 = jnp.bfloat16


def iota(shape, dim):
    return lax.broadcasted_iota(jnp.int32, shape, dim)


def dot(a, b):
    return jnp.dot(a, b, preferred_element_type=F32)


def dot_t(a, b):
    return lax.dot_general(a, b, (((1,), (1,)), ((), ())), preferred_element_type=F32)


def three_parts(x):
    high = x.astype(BF16).astype(F32)
    middle = (x - high).astype(BF16).astype(F32)
    return high, middle, x - high - middle


def pieces_of(columns):
    size = 512 if columns > 1024 else 256
    starts = range(0, columns, size)
    return [(at, min(size, columns - at), "xy"[i] if i < 2 else None) for i, at in enumerate(starts)]


def hand_on(a_ref, b_ref, c_ref, a_out, b_out, c_out):
    a_out[...] = a_ref[...]
    b_out[...] = b_ref[...]
    c_out[...] = c_ref[...]


def kernel(
    nk,
    nh,
    width,
    hid_ref,
    gain_ref,
    post_ref,
    freq_ref,
    wq_hbm,
    wk_hbm,
    wv_hbm,
    wo_hbm,
    wg_hbm,
    wu_hbm,
    wd_hbm,
    keys_hbm,
    values_hbm,
    ctx_ref,
    req_ref,
    start_ref,
    next_ref,
    dkey_ref,
    dval_ref,
    wq,
    wk,
    wv,
    wo,
    wg,
    wu,
    wd,
    keys,
    values,
    hidden_halves,
    send1,
    recv1,
    gath1,
    draft_kv,
    scores,
    runs,
    tops,
    outs,
    sums,
    send2,
    recv2,
    gath2,
    core3,
    along3,
    resid,
    send_sq,
    recv_sq,
    send4,
    recv4,
    line_recv_x,
    line_recv,
    line_sum,
    cross_recv,
    gath4,
    core5,
    along5,
    final,
    local_sem,
    ksend_sem,
    krecv_sem,
    hsend_sem,
    hrecv_sem,
    lsend_sem,
    lrecv_sem,
):
    me_k = lax.axis_index("kvp")
    me_h = lax.axis_index("head")
    nm = nk // 2
    nz = nh // 2
    me_z, core = me_h // 2, me_h % 2
    twin = me_h + 1 - 2 * core

    def along_z(k):
        return lax.rem(me_z + k, nz) * 2 + core

    rows = 8 * nm
    me_m, me_c = me_k // 2, me_k % 2
    side = math.isqrt(nk)
    me_y, me_x = me_k // side, me_k % side
    slots = keys.shape[0]
    db = hid_ref.shape[1]
    half = db // 2
    ff = wg.shape[1]
    fh = ff // 2
    pieces = pieces_of(fh)

    sent = []

    first_copies = [
        pltpu.make_async_copy(src, dst, local_sem.at[i])
        for i, (src, dst) in enumerate([(wq_hbm, wq), (wk_hbm, wk), (wv_hbm, wv)])
    ]
    later_copies = [
        pltpu.make_async_copy(src, dst, local_sem.at[3 + i])
        for i, (src, dst) in enumerate(
            [(keys_hbm, keys), (values_hbm, values), (wo_hbm, wo), (wg_hbm, wg), (wu_hbm, wu), (wd_hbm, wd)]
        )
    ]
    def arrive(i):
        later_copies[i].wait()

    for c in first_copies:
        c.start()

    barrier = pltpu.get_barrier_semaphore()

    offsets = [(dy, dx) for dy in range(side) for dx in range(side) if dy or dx]
    offsets.sort(key=lambda o: -sum(min(d, side - d) for d in o))
    targets = [
        lax.rem(me_y + dy, side) * side + lax.rem(me_x + dx, side) for dy, dx in offsets
    ]
    sources = [
        lax.rem(me_y + side - dy, side) * side + lax.rem(me_x + side - dx, side) for dy, dx in offsets
    ]
    near_first = list(reversed(range(nk - 1)))

    for to in targets:
        pl.semaphore_signal(barrier, inc=1, device_id=(to, me_h), device_id_type=MESH)
    for to in [twin] + [along_z(k) for k in range(1, nz)]:
        pl.semaphore_signal(barrier, inc=1, device_id=(me_k, to), device_id_type=MESH)

    def kvp_copy(phase, i, src, dst):
        return pltpu.make_async_remote_copy(
            src_ref=src,
            dst_ref=dst,
            send_sem=ksend_sem.at[phase, i],
            recv_sem=krecv_sem.at[phase, i],
            device_id=(targets[i], me_h),
            device_id_type=MESH,
        )

    def kvp_start(phase, i, src, dst):
        copy = kvp_copy(phase, i, src, dst)
        copy.start()
        sent.append(copy)

    def head_copy(sem, to, src, dst):
        return pltpu.make_async_remote_copy(
            src_ref=src,
            dst_ref=dst,
            send_sem=hsend_sem.at[sem],
            recv_sem=hrecv_sem.at[sem],
            device_id=(me_k, to),
            device_id_type=MESH,
        )

    def line_copy(sem, k, axis, src, dst):
        if axis == "x":
            to = me_y * side + lax.rem(me_x + k, side)
        else:
            to = lax.rem(me_y + k, side) * side + me_x
        copy = pltpu.make_async_remote_copy(
            src_ref=src,
            dst_ref=dst,
            send_sem=lsend_sem.at[sem, k],
            recv_sem=lrecv_sem.at[sem, k],
            device_id=(to, me_h),
            device_id_type=MESH,
        )
        copy.start()
        sent.append(copy)
        return copy

    def kvp_scatter(phase, send, recv):
        for i, to in enumerate(targets):
            kvp_start(phase, i, send.at[to // 2, to % 2], recv.at[i])

    def kvp_gather(phase, mine):
        for i in range(nk - 1):
            kvp_start(phase, i, mine, mine)

    def kvp_await(phase, i, ref):
        kvp_copy(phase, i, ref, ref).wait_recv()

    def kvp_gather_wait(phase, slot):
        for i in near_first:
            kvp_await(phase, i, slot(sources[i]))

    def kvp_reduce(phase, own, recv):
        total = own.astype(F32)
        for i in near_first:
            kvp_await(phase, i, recv.at[i])
            total = total + recv[i].astype(F32)
        return total

    def halves(x):
        return x[:, :half], x[:, half:]

    def own_half(x):
        left, right = halves(x)
        return jnp.where(core == 0, left, right), jnp.where(core == 0, right, left)

    def head_sum(base, part, swap_ref, along_ref):
        own, other = own_half(part)
        swap_ref[0] = other.astype(BF16)
        swapped = head_copy(base, twin, swap_ref.at[0], swap_ref.at[1])
        swapped.start()
        sent.append(swapped)
        swapped.wait_recv()
        along_ref[0] = (own + swap_ref[1].astype(F32)).astype(BF16)
        copies = [head_copy(base + k, along_z(k), along_ref.at[0], along_ref.at[k]) for k in range(1, nz)]
        for copy in copies:
            copy.start()
        sent.extend(copies)
        for copy in copies:
            copy.wait_recv()
        total = jnp.zeros((rows, half), F32)
        for z in range(nz):
            total = total + along_ref[lax.rem(me_z - z + nz, nz)].astype(F32)
        return total

    def share_half(sem, ref):
        copy = head_copy(sem, twin, ref.at[core], ref.at[core])
        copy.start()
        sent.append(copy)
        copy.wait_recv()

    def finish():
        while sent:
            sent.pop(0).wait_send()

    def folded(x):
        return jnp.concatenate([x[:, : x.shape[1] // 2], x[:, x.shape[1] // 2 :]], axis=0)

    hidden = hid_ref[...].astype(F32)
    hidden_halves[0], hidden_halves[1] = halves(hidden)
    scaled = (hidden * gain_ref[...].astype(F32).reshape(1, db)).astype(BF16)
    square = jnp.sum(hidden * hidden, axis=1, keepdims=True)
    lane = iota((rows, HD), 1)

    def square_tile(column):
        high, middle, low = three_parts(jnp.broadcast_to(column, (rows, HD)))
        return jnp.where(lane == 0, high, jnp.where(lane == 1, middle, jnp.where(lane == 2, low, 0.0)))

    square_in = square_tile(square)
    for c in first_copies:
        c.wait()
    for c in later_copies:
        c.start()
    key_part = dot(scaled, wk[...])
    value_part = dot(scaled, wv[...])
    for c in range(2):
        query_part = dot(scaled, wq[:, c * 512 : (c + 1) * 512])
        upper = query_part[:, :384]
        lower = jnp.concatenate([query_part[:, 384:], value_part if c else key_part, square_in], axis=1)
        send1[:, c] = jnp.concatenate([upper.reshape(nm, 8, 384), lower.reshape(nm, 8, 384)], axis=1).astype(BF16)

    eight = iota((8, HD), 0)
    lane8 = iota((8, HD), 1)
    position = jnp.where(eight < DRAFT, ctx_ref[2 * me_m], ctx_ref[2 * me_m + 1]) + eight % DRAFT
    angle = position.astype(F32) * freq_ref[...]
    cosine = jnp.cos(angle)
    sine = jnp.sin(angle)
    sine = jnp.where(lane8 < HD // 2, -sine, sine)

    def find_last(s, last):
        return jnp.where(lane8 == req_ref[s], s, last)

    last_slots = lax.fori_loop(0, slots, find_last, jnp.full((8, HD), -1, jnp.int32), unroll=8)
    last_of = [jnp.max(jnp.where(lane8 == b, last_slots, -1)) for b in range(nk)]
    pl.semaphore_wait(barrier, nk + nz - 1)
    kvp_scatter(0, send1, recv1)

    total = kvp_reduce(0, send1[me_m, me_c], recv1)
    square_sum = jnp.sum(total[8:, 256:], axis=1, keepdims=True)
    inverse = lax.rsqrt(square_sum / width + EPSILON)
    tiles = [total[:8, :128], total[:8, 128:256], total[:8, 256:], total[8:, :128], total[8:, 128:256]]
    tiles = [t * inverse for t in tiles]
    rotated = [t * cosine + pltpu.roll(t, HD // 2, 1) * sine for t in tiles]
    low_rows = eight < DRAFT

    def swap(x):
        return pltpu.roll(x, DRAFT, 0)

    def first_of(a, b):
        return jnp.where(low_rows, a, swap(b))

    def second_of(a, b):
        return jnp.where(low_rows, swap(a), b)

    q0, q1, q2, q3 = rotated[:4]
    pair = jnp.where(me_c == 0, rotated[4], tiles[4])
    query_slot = gath1.at[pl.ds(2 * me_m, 2), me_c]
    query_slot[0] = jnp.concatenate([first_of(q0, q1), first_of(q2, q3)], axis=0).astype(BF16)
    query_slot[1] = jnp.concatenate([second_of(q0, q1), second_of(q2, q3)], axis=0).astype(BF16)
    draft_kv[me_m, me_c] = jnp.concatenate([pair, jnp.zeros_like(pair)], axis=0).astype(BF16)
    kvp_gather(1, query_slot)
    kv_phase = 5 + 2 * len(pieces)
    kvp_gather(kv_phase, draft_kv.at[me_m, me_c])
    kvp_gather_wait(1, lambda source: gath1.at[pl.ds(2 * (source // 2), 2), source % 2])
    arrive(0)
    token = iota((32, BLOCK), 1)

    def previous(s):
        return req_ref[jnp.maximum(s - 1, 0)]

    def score_step(i, run):
        for u in range(UNROLL):
            s = i * UNROLL + u
            r = req_ref[s]
            safe = jnp.maximum(r, 0)
            live = jnp.where(r >= 0, ctx_ref[safe] - start_ref[s], 0)
            part = jnp.where(token < live, dot_t(gath1[safe].reshape(32, HD), keys[s]), FLOOR)
            scores[s] = part
            run = jnp.maximum(part, jnp.where(r == previous(s), run, FLOOR))
            runs[s] = run
        return run

    floor_tile = jnp.full((32, BLOCK), FLOOR, F32)
    lax.fori_loop(0, slots // UNROLL, score_step, floor_tile)
    for b in range(nk):
        run = runs[jnp.maximum(last_of[b], 0)]
        top = jnp.max(run, axis=1, keepdims=True)
        tops[b] = jnp.where(last_of[b] >= 0, jnp.broadcast_to(top, (32, BLOCK)), FLOOR)

    arrive(1)

    def value_step(i, carry):
        sum_run, out_run = carry
        for u in range(UNROLL):
            s = i * UNROLL + u
            r = req_ref[s]
            keep = jnp.where(r == previous(s), 1.0, 0.0).astype(F32)
            weight = jnp.exp2((scores[s] - tops[jnp.maximum(r, 0)]) * EXP_SCALE)
            sum_run = sum_run * keep + weight
            out_run = out_run * keep + dot(weight.astype(BF16), values[s])
            sums[s] = sum_run
            outs[s] = out_run
        return sum_run, out_run

    zero_tile = jnp.zeros((32, BLOCK), F32)
    lax.fori_loop(0, slots // UNROLL, value_step, (zero_tile, zero_tile))

    lane32 = iota((32, HD), 1)
    stats = zero_tile
    totals = []
    for b in range(nk):
        at = jnp.maximum(last_of[b], 0)
        here = last_of[b] >= 0
        out = jnp.where(here, outs[at], 0.0)
        column = jnp.sum(sums[at], axis=1, keepdims=True)
        totals.append(jnp.where(here, jnp.broadcast_to(column, (32, HD)), 0.0))
        for c in range(2):
            send2[b // 2, c, 16 * (b % 2) : 16 * (b % 2) + 16, :] = out[16 * c : 16 * c + 16].astype(BF16)
    for m in range(nm):
        for c in range(2):
            j = 2 * m + c
            part = slice(16 * c, 16 * c + 16)
            top = jnp.concatenate([tops[2 * m, part], tops[2 * m + 1, part]], axis=0)
            summed = jnp.concatenate([totals[2 * m][part], totals[2 * m + 1][part]], axis=0)
            stats = jnp.where(lane32 // 8 == j, jnp.where(lane32 % 8 < 3, top, summed), stats)
    high, middle, low = three_parts(stats)
    kind = lane32 % 8
    stats = jnp.where(
        kind % 3 == 0, high, jnp.where(kind % 3 == 1, middle, low)
    )
    stats = jnp.where(kind < 6, stats, 0.0)
    turned = jnp.concatenate([stats, jnp.zeros((HD - 32, HD), F32)], axis=0).T
    for m in range(nm):
        for c in range(2):
            j = 2 * m + c
            tile = jnp.concatenate([turned[8 * j : 8 * j + 8], jnp.zeros((8, HD), F32)], axis=0)
            send2[m, c, 32:48, :] = tile.astype(BF16)
    kvp_scatter(2, send2, recv2)

    finish()
    kvp_gather_wait(kv_phase, lambda source: draft_kv.at[source // 2, source % 2])
    for c, out_ref in enumerate((dkey_ref, dval_ref)):
        out_ref[...] = jnp.concatenate([draft_kv[m, c].astype(F32)[:8] for m in range(nm)], axis=0).astype(BF16)
    mine = gath1[pl.ds(2 * me_m, 2), me_c].reshape(32, HD)
    draft_score = dot_t(mine, draft_kv[me_m, 0])
    row16, col16 = iota((32, 16), 0), iota((32, 16), 1)
    seen = (col16 // DRAFT == row16 // 16) & (col16 % DRAFT <= row16 % DRAFT)
    draft_score = jnp.where(seen, draft_score, FLOOR)
    draft_top = jnp.max(draft_score, axis=1, keepdims=True)
    draft_weight = jnp.where(seen, jnp.exp2((draft_score - draft_top) * EXP_SCALE), 0.0)
    draft_sum = jnp.sum(draft_weight, axis=1, keepdims=True)
    draft_out = dot(draft_weight.astype(BF16), draft_kv[me_m, 1])

    for i in near_first:
        kvp_await(2, i, recv2.at[i])
    partials = [send2.at[me_m, me_c]] + [recv2.at[i] for i in range(nk - 1)]
    every = [p[32:48, :].astype(F32)[:8] for p in partials]
    every = jnp.concatenate(every + [jnp.zeros((8, HD), F32)] * (HD // 8 - nk), axis=0)
    turned = every.T[:32]
    joined = turned + pltpu.roll(turned, HD - 1, 1) + pltpu.roll(turned, HD - 2, 1)
    own_lane = (lane32 % 8 == 0) & (lane32 < 8 * nk)
    peak = jnp.max(jnp.where(own_lane, joined, FLOOR), axis=1, keepdims=True)
    peak = jnp.maximum(peak, draft_top)
    factor = jnp.where(own_lane, jnp.exp2((joined - peak) * EXP_SCALE), 0.0)
    whole = jnp.where(own_lane, factor * pltpu.roll(joined, HD - 3, 1), 0.0)
    draft_factor = jnp.exp2((draft_top - peak) * EXP_SCALE)
    whole = jnp.sum(whole, axis=1, keepdims=True) + draft_sum * draft_factor
    factor = factor / whole
    mixed = draft_out * (draft_factor / whole)
    for i in range(nk):
        mixed = mixed + partials[i][:32, :].astype(F32) * factor[:, 8 * i : 8 * i + 1]
    a0, a1, b0, b1 = mixed[:8], mixed[8:16], mixed[16:24], mixed[24:]
    h0, h1 = first_of(a0, b0), second_of(a0, b0)
    h2, h3 = first_of(a1, b1), second_of(a1, b1)
    gath2[me_m, me_c] = jnp.concatenate(
        [jnp.concatenate([h0, h1], axis=1), jnp.concatenate([h2, h3], axis=1)], axis=0
    ).astype(BF16)
    kvp_gather(3, gath2.at[me_m, me_c])
    finish()
    arrive(2)
    kvp_gather_wait(3, lambda source: gath2.at[source // 2, source % 2])

    attn_part = jnp.zeros((rows, db), F32)
    for c in range(2):
        for g in range(2):
            piece = jnp.concatenate(
                [gath2[m, c].astype(F32)[8 * g : 8 * g + 8] for m in range(nm)], axis=0
            ).astype(BF16)
            attn_part += dot(piece, wo[512 * c + 256 * g : 512 * c + 256 * g + 256, :])
    attn = head_sum(0, attn_part, core3, along3)
    resid[core] = (hidden_halves[core] + attn).astype(BF16)
    share_half(nz, resid)
    residual = jnp.concatenate([resid[0].astype(F32), resid[1].astype(F32)], axis=1)
    normed = (residual * post_ref[...].astype(F32).reshape(1, db)).astype(BF16)
    arrive(3)
    arrive(4)
    lines, direct = {}, []
    for p, (at, size, axis) in enumerate(pieces):
        part = pl.ds(at, size)
        for c in range(2):
            columns = slice(c * fh + at, c * fh + at + size)
            gate = dot(normed, wg[:, columns]).reshape(nm, 8, size)
            up = dot(normed, wu[:, columns]).reshape(nm, 8, size)
            both = jnp.concatenate([gate, up], axis=1).astype(BF16)
            send4[:, :, c, :, part] = both.reshape(side, side // 2, 16, size)
        if axis is None:
            direct.append((p, part))
            continue
        lines[p] = []
        for k in [side // 2] + [k for k in range(1, side) if k != side // 2]:
            if axis == "x":
                x = lax.rem(me_x + k, side)
                src, dst = send4.at[:, x // 2, x % 2, :, part], line_recv_x.at[k - 1, :, :, part]
            else:
                y = lax.rem(me_y + k, side)
                src, dst = send4.at[y, :, :, :, part], line_recv.at[k - 1, :, :, :, part]
            lines[p].append(line_copy(p, k, axis, src, dst))
        if p == 0:
            square_out = square_tile(jnp.sum(residual * residual, axis=1, keepdims=True)).reshape(nm, 8, HD)
            square_out = jnp.concatenate([square_out, jnp.zeros_like(square_out)], axis=1).astype(BF16)
            send_sq[:, 0] = square_out
            send_sq[:, 1] = square_out
            kvp_scatter(4, send_sq, recv_sq)
    finish()
    for p, part in direct:
        for i, to in enumerate(targets):
            src = send4.at[to // side, (to % side) // 2, to % 2, :, part]
            kvp_start(5 + p, i, src, recv4.at[i, :, part])
    crossing = {}
    for p, (at, size, axis) in enumerate(pieces):
        if axis is None:
            continue
        part = pl.ds(at, size)
        for copy in lines[p]:
            copy.wait_recv()
        if axis == "x":
            own, here = send4[:, me_x // 2, me_x % 2, :, part], me_y
        else:
            own, here = send4[me_y, :, :, :, part].reshape(side, 16, size), me_x
        total = own.astype(F32)
        for k in range(1, side):
            if axis == "x":
                total = total + line_recv_x[k - 1, :, :, part].astype(F32)
            else:
                total = total + line_recv[k - 1, :, :, :, part].astype(F32).reshape(side, 16, size)
        line_sum[:, :, part] = total.astype(BF16)
        crossing[p] = [
            line_copy(
                2 + p,
                k,
                "y" if axis == "x" else "x",
                line_sum.at[lax.rem(here + k, side), :, part],
                cross_recv.at[k - 1, :, part],
            )
            for k in range(1, side)
        ]
    total = kvp_reduce(4, send_sq[me_m, me_c], recv_sq)
    inverse = lax.rsqrt(jnp.sum(total[:8], axis=1, keepdims=True) / width + EPSILON)
    base = 5 + len(pieces)
    for p, (at, size, axis) in enumerate(pieces):
        part = pl.ds(at, size)
        if axis is None:
            own = send4[me_y, me_x // 2, me_c, :, part]
            total = kvp_reduce(5 + p, own, recv4.at[:, :, part])
        else:
            for copy in crossing[p]:
                copy.wait_recv()
            total = line_sum[me_y if axis == "x" else me_x, :, part].astype(F32)
            for k in range(1, side):
                total = total + cross_recv[k - 1, :, part].astype(F32)
        gate = total[:8] * inverse
        up = total[8:] * inverse
        middle = gate / (1.0 + jnp.exp(-gate)) * up
        mine = gath4.at[me_m, me_c, :, pl.ds(at // 2, size // 2)]
        mine[...] = folded(middle).astype(BF16)
        kvp_gather(base + p, mine)
    finish()
    arrive(5)
    down_part = jnp.zeros((rows, db), F32)
    for p, (at, size, _) in enumerate(pieces):
        part = pl.ds(at // 2, size // 2)
        kvp_gather_wait(base + p, lambda source, part=part: gath4.at[source // 2, source % 2, :, part])
        for c in range(2):
            rows_of = [gath4[m, c, :, part].astype(F32) for m in range(nm)]
            piece = jnp.concatenate(
                [jnp.concatenate([r[:8] for r in rows_of], axis=0), jnp.concatenate([r[8:] for r in rows_of], axis=0)],
                axis=1,
            ).astype(BF16)
            down_part += dot(piece, wd[c * fh + at : c * fh + at + size, :])
    down = head_sum(nz + 1, down_part, core5, along5)
    final[core] = (resid[core].astype(F32) + down).astype(BF16)
    share_half(2 * nz + 1, final)
    next_ref[:, :half] = final[0]
    next_ref[:, half:] = final[1]
    finish()


def body(
    nk,
    nh,
    hidden_in,
    norm_gain,
    w_query,
    w_key,
    w_value,
    w_out,
    post_gain,
    w_gate,
    w_up,
    w_down,
    cache_keys,
    cache_values,
    context_len,
    slot_request,
    slot_start,
):
    rows, db = hidden_in.shape
    nm = nk // 2
    slots = cache_keys.shape[0]
    fh = w_gate.shape[1] // 2
    half, nz, side, count = db // 2, nh // 2, math.isqrt(nk), len(pieces_of(fh))
    exponent = np.arange(HD // 2, dtype=np.float32) * np.float32(2.0 / HD)
    frequency = (THETA_BASE ** (-exponent.astype(np.float64))).astype(np.float32)
    frequency = jnp.asarray(np.concatenate([frequency, frequency])[None, :])
    vmem = pl.BlockSpec(memory_space=pltpu.VMEM)
    hbm = pl.BlockSpec(memory_space=pl.ANY)
    smem = pl.BlockSpec(memory_space=pltpu.SMEM)
    scratch = [
        pltpu.VMEM(w.shape, BF16)
        for w in (w_query, w_key, w_value, w_out, w_gate, w_up, w_down, cache_keys, cache_values)
    ]
    scratch += [
        pltpu.VMEM((2, rows, half), F32),
        pltpu.VMEM((nm, 2, 16, 384), BF16),
        pltpu.VMEM((nk - 1, 16, 384), BF16),
        pltpu.VMEM((nk, 2, 16, HD), BF16),
        pltpu.VMEM((nm, 2, 16, HD), BF16),
        pltpu.VMEM((slots, 32, BLOCK), F32),
        pltpu.VMEM((slots, 32, BLOCK), F32),
        pltpu.VMEM((nk, 32, BLOCK), F32),
        pltpu.VMEM((slots, 32, HD), F32),
        pltpu.VMEM((slots, 32, BLOCK), F32),
        pltpu.VMEM((nm, 2, 48, HD), BF16),
        pltpu.VMEM((nk - 1, 48, HD), BF16),
        pltpu.VMEM((nm, 2, 16, 256), BF16),
        pltpu.VMEM((2, rows, half), BF16),
        pltpu.VMEM((nz, rows, half), BF16),
        pltpu.VMEM((2, rows, half), BF16),
        pltpu.VMEM((nm, 2, 16, HD), BF16),
        pltpu.VMEM((nk - 1, 16, HD), BF16),
        pltpu.VMEM((side, side // 2, 2, 16, fh), BF16),
        pltpu.VMEM((nk - 1, 16, fh), BF16),
        pltpu.VMEM((side - 1, side, 16, fh), BF16),
        pltpu.VMEM((side - 1, side // 2, 2, 16, fh), BF16),
        pltpu.VMEM((side, 16, fh), BF16),
        pltpu.VMEM((side - 1, 16, fh), BF16),
        pltpu.VMEM((nm, 2, 16, fh // 2), BF16),
        pltpu.VMEM((2, rows, half), BF16),
        pltpu.VMEM((nz, rows, half), BF16),
        pltpu.VMEM((2, rows, half), BF16),
        pltpu.SemaphoreType.DMA((9,)),
        pltpu.SemaphoreType.DMA((6 + 2 * count, nk)),
        pltpu.SemaphoreType.DMA((6 + 2 * count, nk)),
        pltpu.SemaphoreType.DMA((2 * nz + 2,)),
        pltpu.SemaphoreType.DMA((2 * nz + 2,)),
        pltpu.SemaphoreType.DMA((4, side)),
        pltpu.SemaphoreType.DMA((4, side)),
    ]
    weight_items = sum(w.size for w in (w_query, w_key, w_value, w_out, w_gate, w_up, w_down))
    results = pl.pallas_call(
        functools.partial(kernel, nk, nh, db * nk),
        out_shape=(
            jax.ShapeDtypeStruct((rows, db), BF16),
            jax.ShapeDtypeStruct((rows, HD), BF16),
            jax.ShapeDtypeStruct((rows, HD), BF16),
        ),
        in_specs=[vmem] * 4 + [hbm] * 9 + [smem] * 3,
        out_specs=(vmem, vmem, vmem),
        scratch_shapes=scratch,
        compiler_params=pltpu.CompilerParams(
            collective_id=0, has_side_effects=True, vmem_limit_bytes=56 * 1024 * 1024
        ),
        cost_estimate=pl.CostEstimate(
            flops=2 * rows * weight_items + 4 * slots * 32 * BLOCK * HD,
            bytes_accessed=2 * (weight_items + 2 * cache_keys.size),
            transcendentals=slots * 32 * BLOCK,
        ),
    )(
        hidden_in,
        norm_gain,
        post_gain,
        frequency,
        w_query,
        w_key,
        w_value,
        w_out,
        w_gate,
        w_up,
        w_down,
        cache_keys,
        cache_values,
        context_len,
        slot_request,
        slot_start,
    )
    return pl.pallas_call(
        hand_on,
        out_shape=tuple(jax.ShapeDtypeStruct(r.shape, r.dtype) for r in results),
        in_specs=[vmem] * 3,
        out_specs=(vmem,) * 3,
    )(*results)


def solution(mesh):
    return jax.shard_map(
        functools.partial(body, mesh.shape["kvp"], mesh.shape["head"]),
        mesh=mesh,
        in_specs=(
            P(None, "kvp"),
            P("kvp"),
            P("kvp", "head"),
            P("kvp", "head"),
            P("kvp", "head"),
            P("head", "kvp"),
            P("kvp"),
            P("kvp", "head"),
            P("kvp", "head"),
            P("head", "kvp"),
            P("kvp", None, "head"),
            P("kvp", None, "head"),
            P(),
            P("kvp"),
            P("kvp"),
        ),
        out_specs=(P(None, "kvp"), P(None, "head"), P(None, "head")),
        check_vma=False,
    )
```

```python
import functools
import math

import jax
import jax.numpy as jnp
import numpy as np
from jax import lax
from jax.experimental import pallas as pl
from jax.experimental.pallas import tpu as pltpu
from jax.sharding import PartitionSpec as P

HD = 128
DRAFT = 4
BLOCK = 128
EPSILON = 1e-05
THETA_BASE = 500000.0
FLOOR = -1e30
LOG2E = math.log2(math.e)
EXP_SCALE = LOG2E / math.sqrt(HD)
UNROLL = 80
MESH = pl.DeviceIdType.MESH
F32 = jnp.float32
BF16 = jnp.bfloat16


def iota(shape, dim):
    return lax.broadcasted_iota(jnp.int32, shape, dim)


def dot(a, b):
    return jnp.dot(a, b, preferred_element_type=F32)


def dot_t(a, b):
    return lax.dot_general(a, b, (((1,), (1,)), ((), ())), preferred_element_type=F32)


def three_parts(x):
    high = x.astype(BF16).astype(F32)
    middle = (x - high).astype(BF16).astype(F32)
    return high, middle, x - high - middle


def pieces_of(columns):
    size = max(256, columns * 3 // 7 // 256 * 256)
    return [(0, size, "x"), (size, size, "y"), (2 * size, columns - 2 * size, None)]


def hand_on(a_ref, b_ref, c_ref, a_out, b_out, c_out):
    a_out[...] = a_ref[...]
    b_out[...] = b_ref[...]
    c_out[...] = c_ref[...]


def kernel(
    nk,
    nh,
    width,
    hid_ref,
    gain_ref,
    post_ref,
    freq_ref,
    wq_hbm,
    wk_hbm,
    wv_hbm,
    wo_hbm,
    wg_hbm,
    wu_hbm,
    wd_hbm,
    keys_hbm,
    values_hbm,
    ctx_ref,
    req_ref,
    start_ref,
    next_ref,
    dkey_ref,
    dval_ref,
    wq,
    wk,
    wv,
    wo,
    wg,
    wu,
    wd,
    keys,
    values,
    hidden_halves,
    send1,
    recv1,
    gath1,
    draft_kv,
    turned_keys,
    scores,
    runs,
    tops,
    outs,
    sums,
    send2,
    recv2,
    gath2,
    core3,
    along3,
    resid,
    send_sq,
    recv_sq,
    send4,
    recv4,
    line_recv_x,
    line_recv,
    line_sum,
    cross_recv,
    gath4,
    core5,
    along5,
    final,
    local_sem,
    ksend_sem,
    krecv_sem,
    hsend_sem,
    hrecv_sem,
    lsend_sem,
    lrecv_sem,
):
    me_k = lax.axis_index("kvp")
    me_h = lax.axis_index("head")
    nm = nk // 2
    nz = nh // 2
    me_z, core = me_h // 2, me_h % 2
    twin = me_h + 1 - 2 * core

    def along_z(k):
        return lax.rem(me_z + k, nz) * 2 + core

    rows = 8 * nm
    me_m, me_c = me_k // 2, me_k % 2
    side = math.isqrt(nk)
    me_y, me_x = me_k // side, me_k % side
    slots = keys.shape[0]
    db = hid_ref.shape[1]
    half = db // 2
    ff = wg.shape[1]
    fh = ff // 2
    pieces = pieces_of(fh)

    sent = []

    first_copies = [
        pltpu.make_async_copy(src, dst, local_sem.at[i])
        for i, (src, dst) in enumerate([(wq_hbm, wq), (wk_hbm, wk), (wv_hbm, wv)])
    ]
    later_copies = [
        pltpu.make_async_copy(src, dst, local_sem.at[3 + i])
        for i, (src, dst) in enumerate(
            [(keys_hbm, keys), (values_hbm, values), (wo_hbm, wo), (wg_hbm, wg), (wu_hbm, wu), (wd_hbm, wd)]
        )
    ]
    def arrive(i):
        later_copies[i].wait()

    for c in first_copies:
        c.start()

    barrier = pltpu.get_barrier_semaphore()

    offsets = [(dy, dx) for dy in range(side) for dx in range(side) if dy or dx]
    offsets.sort(key=lambda o: -sum(min(d, side - d) for d in o))
    targets = [
        lax.rem(me_y + dy, side) * side + lax.rem(me_x + dx, side) for dy, dx in offsets
    ]
    sources = [
        lax.rem(me_y + side - dy, side) * side + lax.rem(me_x + side - dx, side) for dy, dx in offsets
    ]
    near_first = list(reversed(range(nk - 1)))

    for to in targets:
        pl.semaphore_signal(barrier, inc=1, device_id=(to, me_h), device_id_type=MESH)
    for to in [twin] + [along_z(k) for k in range(1, nz)]:
        pl.semaphore_signal(barrier, inc=1, device_id=(me_k, to), device_id_type=MESH)

    def kvp_copy(phase, i, src, dst):
        return pltpu.make_async_remote_copy(
            src_ref=src,
            dst_ref=dst,
            send_sem=ksend_sem.at[phase, i],
            recv_sem=krecv_sem.at[phase, i],
            device_id=(targets[i], me_h),
            device_id_type=MESH,
        )

    def kvp_start(phase, i, src, dst):
        copy = kvp_copy(phase, i, src, dst)
        copy.start()
        sent.append(copy)

    def head_copy(sem, to, src, dst):
        return pltpu.make_async_remote_copy(
            src_ref=src,
            dst_ref=dst,
            send_sem=hsend_sem.at[sem],
            recv_sem=hrecv_sem.at[sem],
            device_id=(me_k, to),
            device_id_type=MESH,
        )

    def line_copy(sem, k, axis, src, dst):
        if axis == "x":
            to = me_y * side + lax.rem(me_x + k, side)
        else:
            to = lax.rem(me_y + k, side) * side + me_x
        copy = pltpu.make_async_remote_copy(
            src_ref=src,
            dst_ref=dst,
            send_sem=lsend_sem.at[sem, k],
            recv_sem=lrecv_sem.at[sem, k],
            device_id=(to, me_h),
            device_id_type=MESH,
        )
        copy.start()
        sent.append(copy)
        return copy

    def kvp_scatter(phase, send, recv):
        for i, to in enumerate(targets):
            kvp_start(phase, i, send.at[to // 2, to % 2], recv.at[i])

    def kvp_gather(phase, mine):
        for i in range(nk - 1):
            kvp_start(phase, i, mine, mine)

    def kvp_await(phase, i, ref):
        kvp_copy(phase, i, ref, ref).wait_recv()

    def kvp_gather_wait(phase, slot):
        for i in near_first:
            kvp_await(phase, i, slot(sources[i]))

    def kvp_reduce(phase, own, recv):
        total = own.astype(F32)
        for i in near_first:
            kvp_await(phase, i, recv.at[i])
            total = total + recv[i].astype(F32)
        return total

    def halves(x):
        return x[:, :half], x[:, half:]

    def own_half(x):
        left, right = halves(x)
        return jnp.where(core == 0, left, right), jnp.where(core == 0, right, left)

    def head_sum(base, part, swap_ref, along_ref):
        own, other = own_half(part)
        swap_ref[0] = other.astype(BF16)
        swapped = head_copy(base, twin, swap_ref.at[0], swap_ref.at[1])
        swapped.start()
        sent.append(swapped)
        swapped.wait_recv()
        along_ref[0] = (own + swap_ref[1].astype(F32)).astype(BF16)
        copies = [head_copy(base + k, along_z(k), along_ref.at[0], along_ref.at[k]) for k in range(1, nz)]
        for copy in copies:
            copy.start()
        sent.extend(copies)
        for copy in copies:
            copy.wait_recv()
        total = jnp.zeros((rows, half), F32)
        for z in range(nz):
            total = total + along_ref[lax.rem(me_z - z + nz, nz)].astype(F32)
        return total

    def share_half(sem, ref):
        copy = head_copy(sem, twin, ref.at[core], ref.at[core])
        copy.start()
        sent.append(copy)
        copy.wait_recv()

    def finish():
        while sent:
            sent.pop(0).wait_send()

    def folded(x):
        return jnp.concatenate([x[:, : x.shape[1] // 2], x[:, x.shape[1] // 2 :]], axis=0)

    hidden = hid_ref[...].astype(F32)
    hidden_halves[0], hidden_halves[1] = halves(hidden)
    scaled = (hidden * gain_ref[...].astype(F32).reshape(1, db)).astype(BF16)
    square = jnp.sum(hidden * hidden, axis=1, keepdims=True)
    lane = iota((rows, HD), 1)

    def square_tile(column):
        high, middle, low = three_parts(jnp.broadcast_to(column, (rows, HD)))
        return jnp.where(lane == 0, high, jnp.where(lane == 1, middle, jnp.where(lane == 2, low, 0.0)))

    square_in = square_tile(square)
    for c in first_copies:
        c.wait()
    for c in later_copies:
        c.start()
    key_part = dot(scaled, wk[...])
    value_part = dot(scaled, wv[...])
    for c in range(2):
        query_part = dot(scaled, wq[:, c * 512 : (c + 1) * 512])
        upper = query_part[:, :384]
        lower = jnp.concatenate([query_part[:, 384:], value_part if c else key_part, square_in], axis=1)
        send1[:, c] = jnp.concatenate([upper.reshape(nm, 8, 384), lower.reshape(nm, 8, 384)], axis=1).astype(BF16)

    eight = iota((8, HD), 0)
    lane8 = iota((8, HD), 1)
    position = jnp.where(eight < DRAFT, ctx_ref[2 * me_m], ctx_ref[2 * me_m + 1]) + eight % DRAFT
    angle = position.astype(F32) * freq_ref[...]
    cosine = jnp.cos(angle)
    sine = jnp.sin(angle)
    sine = jnp.where(lane8 < HD // 2, -sine, sine)

    def find_last(s, last):
        return jnp.where(lane8 == req_ref[s], s, last)

    last_slots = lax.fori_loop(0, slots, find_last, jnp.full((8, HD), -1, jnp.int32), unroll=8)
    last_of = [jnp.max(jnp.where(lane8 == b, last_slots, -1)) for b in range(nk)]
    pl.semaphore_wait(barrier, nk + nz - 1)
    kvp_scatter(0, send1, recv1)

    arrive(0)

    def turn_keys(i, _):
        for u in range(4):
            n = 4 * i + u
            turned_keys[n, :, :BLOCK] = keys[2 * n].T
            turned_keys[n, :, BLOCK:] = keys[2 * n + 1].T
        return 0

    lax.fori_loop(0, slots // 8, turn_keys, 0)
    total = kvp_reduce(0, send1[me_m, me_c], recv1)
    square_sum = jnp.sum(total[8:, 256:], axis=1, keepdims=True)
    inverse = lax.rsqrt(square_sum / width + EPSILON)
    tiles = [total[:8, :128], total[:8, 128:256], total[:8, 256:], total[8:, :128], total[8:, 128:256]]
    tiles = [t * inverse for t in tiles]
    rotated = [t * cosine + pltpu.roll(t, HD // 2, 1) * sine for t in tiles]
    low_rows = eight < DRAFT

    def swap(x):
        return pltpu.roll(x, DRAFT, 0)

    def first_of(a, b):
        return jnp.where(low_rows, a, swap(b))

    def second_of(a, b):
        return jnp.where(low_rows, swap(a), b)

    q0, q1, q2, q3 = rotated[:4]
    pair = jnp.where(me_c == 0, rotated[4], tiles[4])
    query_slot = gath1.at[pl.ds(2 * me_m, 2), me_c]
    query_slot[0] = jnp.concatenate([first_of(q0, q1), first_of(q2, q3)], axis=0).astype(BF16)
    query_slot[1] = jnp.concatenate([second_of(q0, q1), second_of(q2, q3)], axis=0).astype(BF16)
    draft_kv[me_m, me_c] = jnp.concatenate([pair, jnp.zeros_like(pair)], axis=0).astype(BF16)
    kvp_gather(1, query_slot)
    kv_phase = 5 + 2 * len(pieces)
    kvp_gather(kv_phase, draft_kv.at[me_m, me_c])
    kvp_gather_wait(1, lambda source: gath1.at[pl.ds(2 * (source // 2), 2), source % 2])
    token = iota((32, BLOCK), 1)

    def previous(s):
        return req_ref[jnp.maximum(s - 1, 0)]

    def score_step(i, run):
        for u in range(0, UNROLL, 2):
            s = i * UNROLL + u
            request = [req_ref[s], req_ref[s + 1]]
            safe = [jnp.maximum(r, 0) for r in request]
            both = jnp.concatenate([gath1[r].reshape(32, HD) for r in safe], axis=0)
            product = dot(both, turned_keys[i * (UNROLL // 2) + u // 2])
            for v in range(2):
                r = request[v]
                live = jnp.where(r >= 0, ctx_ref[safe[v]] - start_ref[s + v], 0)
                part = product[32 * v : 32 * v + 32, BLOCK * v : BLOCK * v + BLOCK]
                part = jnp.where(token < live, part, FLOOR)
                scores[s + v] = part
                run = jnp.maximum(part, jnp.where(r == previous(s + v), run, FLOOR))
                runs[s + v] = run
        return run

    floor_tile = jnp.full((32, BLOCK), FLOOR, F32)
    lax.fori_loop(0, slots // UNROLL, score_step, floor_tile)
    for b in range(nk):
        run = runs[jnp.maximum(last_of[b], 0)]
        top = jnp.max(run, axis=1, keepdims=True)
        tops[b] = jnp.where(last_of[b] >= 0, jnp.broadcast_to(top, (32, BLOCK)), FLOOR)

    arrive(1)

    def value_step(i, carry):
        sum_run, out_run = carry
        for u in range(0, UNROLL, 2):
            s = i * UNROLL + u
            weight = [
                jnp.exp2((scores[s + v] - tops[jnp.maximum(req_ref[s + v], 0)]) * EXP_SCALE) for v in range(2)
            ]
            product = dot(
                jnp.concatenate(weight, axis=0).astype(BF16), jnp.concatenate([values[s], values[s + 1]], axis=1)
            )
            for v in range(2):
                keep = jnp.where(req_ref[s + v] == previous(s + v), 1.0, 0.0).astype(F32)
                sum_run = sum_run * keep + weight[v]
                out_run = out_run * keep + product[32 * v : 32 * v + 32, HD * v : HD * v + HD]
                sums[s + v] = sum_run
                outs[s + v] = out_run
        return sum_run, out_run

    zero_tile = jnp.zeros((32, BLOCK), F32)
    lax.fori_loop(0, slots // UNROLL, value_step, (zero_tile, zero_tile))

    lane32 = iota((32, HD), 1)
    stats = zero_tile
    totals = []
    for b in range(nk):
        at = jnp.maximum(last_of[b], 0)
        here = last_of[b] >= 0
        out = jnp.where(here, outs[at], 0.0)
        column = jnp.sum(sums[at], axis=1, keepdims=True)
        totals.append(jnp.where(here, jnp.broadcast_to(column, (32, HD)), 0.0))
        for c in range(2):
            send2[b // 2, c, 16 * (b % 2) : 16 * (b % 2) + 16, :] = out[16 * c : 16 * c + 16].astype(BF16)
    for m in range(nm):
        for c in range(2):
            j = 2 * m + c
            part = slice(16 * c, 16 * c + 16)
            top = jnp.concatenate([tops[2 * m, part], tops[2 * m + 1, part]], axis=0)
            summed = jnp.concatenate([totals[2 * m][part], totals[2 * m + 1][part]], axis=0)
            stats = jnp.where(lane32 // 8 == j, jnp.where(lane32 % 8 < 3, top, summed), stats)
    high, middle, low = three_parts(stats)
    kind = lane32 % 8
    stats = jnp.where(
        kind % 3 == 0, high, jnp.where(kind % 3 == 1, middle, low)
    )
    stats = jnp.where(kind < 6, stats, 0.0)
    turned = jnp.concatenate([stats, jnp.zeros((HD - 32, HD), F32)], axis=0).T
    for m in range(nm):
        for c in range(2):
            j = 2 * m + c
            tile = jnp.concatenate([turned[8 * j : 8 * j + 8], jnp.zeros((8, HD), F32)], axis=0)
            send2[m, c, 32:48, :] = tile.astype(BF16)
    kvp_scatter(2, send2, recv2)

    finish()
    kvp_gather_wait(kv_phase, lambda source: draft_kv.at[source // 2, source % 2])
    for c, out_ref in enumerate((dkey_ref, dval_ref)):
        out_ref[...] = jnp.concatenate([draft_kv[m, c].astype(F32)[:8] for m in range(nm)], axis=0).astype(BF16)
    mine = gath1[pl.ds(2 * me_m, 2), me_c].reshape(32, HD)
    draft_score = dot_t(mine, draft_kv[me_m, 0])
    row16, col16 = iota((32, 16), 0), iota((32, 16), 1)
    seen = (col16 // DRAFT == row16 // 16) & (col16 % DRAFT <= row16 % DRAFT)
    draft_score = jnp.where(seen, draft_score, FLOOR)
    draft_top = jnp.max(draft_score, axis=1, keepdims=True)
    draft_weight = jnp.where(seen, jnp.exp2((draft_score - draft_top) * EXP_SCALE), 0.0)
    draft_sum = jnp.sum(draft_weight, axis=1, keepdims=True)
    draft_out = dot(draft_weight.astype(BF16), draft_kv[me_m, 1])

    for i in near_first:
        kvp_await(2, i, recv2.at[i])
    partials = [send2.at[me_m, me_c]] + [recv2.at[i] for i in range(nk - 1)]
    every = [p[32:48, :].astype(F32)[:8] for p in partials]
    every = jnp.concatenate(every + [jnp.zeros((8, HD), F32)] * (HD // 8 - nk), axis=0)
    turned = every.T[:32]
    joined = turned + pltpu.roll(turned, HD - 1, 1) + pltpu.roll(turned, HD - 2, 1)
    own_lane = (lane32 % 8 == 0) & (lane32 < 8 * nk)
    peak = jnp.max(jnp.where(own_lane, joined, FLOOR), axis=1, keepdims=True)
    peak = jnp.maximum(peak, draft_top)
    factor = jnp.where(own_lane, jnp.exp2((joined - peak) * EXP_SCALE), 0.0)
    whole = jnp.where(own_lane, factor * pltpu.roll(joined, HD - 3, 1), 0.0)
    draft_factor = jnp.exp2((draft_top - peak) * EXP_SCALE)
    whole = jnp.sum(whole, axis=1, keepdims=True) + draft_sum * draft_factor
    factor = factor / whole
    mixed = draft_out * (draft_factor / whole)
    for i in range(nk):
        mixed = mixed + partials[i][:32, :].astype(F32) * factor[:, 8 * i : 8 * i + 1]
    a0, a1, b0, b1 = mixed[:8], mixed[8:16], mixed[16:24], mixed[24:]
    h0, h1 = first_of(a0, b0), second_of(a0, b0)
    h2, h3 = first_of(a1, b1), second_of(a1, b1)
    gath2[me_m, me_c] = jnp.concatenate(
        [jnp.concatenate([h0, h1], axis=1), jnp.concatenate([h2, h3], axis=1)], axis=0
    ).astype(BF16)
    kvp_gather(3, gath2.at[me_m, me_c])
    finish()
    arrive(2)
    kvp_gather_wait(3, lambda source: gath2.at[source // 2, source % 2])

    attn_part = jnp.zeros((rows, db), F32)
    for c in range(2):
        for g in range(2):
            piece = jnp.concatenate(
                [gath2[m, c].astype(F32)[8 * g : 8 * g + 8] for m in range(nm)], axis=0
            ).astype(BF16)
            attn_part += dot(piece, wo[512 * c + 256 * g : 512 * c + 256 * g + 256, :])
    attn = head_sum(0, attn_part, core3, along3)
    resid[core] = (hidden_halves[core] + attn).astype(BF16)
    share_half(nz, resid)
    residual = jnp.concatenate([resid[0].astype(F32), resid[1].astype(F32)], axis=1)
    normed = (residual * post_ref[...].astype(F32).reshape(1, db)).astype(BF16)
    arrive(3)
    arrive(4)
    lines, direct = {}, []
    for p, (at, size, axis) in enumerate(pieces):
        part = pl.ds(at, size)
        for c in range(2):
            columns = slice(c * fh + at, c * fh + at + size)
            gate = dot(normed, wg[:, columns]).reshape(nm, 8, size)
            up = dot(normed, wu[:, columns]).reshape(nm, 8, size)
            both = jnp.concatenate([gate, up], axis=1).astype(BF16)
            send4[:, :, c, :, part] = both.reshape(side, side // 2, 16, size)
        if axis is None:
            direct.append((p, part))
            continue
        lines[p] = []
        for k in [side // 2] + [k for k in range(1, side) if k != side // 2]:
            if axis == "x":
                x = lax.rem(me_x + k, side)
                src, dst = send4.at[:, x // 2, x % 2, :, part], line_recv_x.at[k - 1, :, :, part]
            else:
                y = lax.rem(me_y + k, side)
                src, dst = send4.at[y, :, :, :, part], line_recv.at[k - 1, :, :, :, part]
            lines[p].append(line_copy(p, k, axis, src, dst))
        if p == 0:
            square_out = square_tile(jnp.sum(residual * residual, axis=1, keepdims=True)).reshape(nm, 8, HD)
            square_out = jnp.concatenate([square_out, jnp.zeros_like(square_out)], axis=1).astype(BF16)
            send_sq[:, 0] = square_out
            send_sq[:, 1] = square_out
            kvp_scatter(4, send_sq, recv_sq)
    finish()
    for p, part in direct:
        for i, to in enumerate(targets):
            src = send4.at[to // side, (to % side) // 2, to % 2, :, part]
            kvp_start(5 + p, i, src, recv4.at[i, :, part])
    crossing = {}
    for p, (at, size, axis) in enumerate(pieces):
        if axis is None:
            continue
        part = pl.ds(at, size)
        for copy in lines[p]:
            copy.wait_recv()
        if axis == "x":
            own, here = send4[:, me_x // 2, me_x % 2, :, part], me_y
        else:
            own, here = send4[me_y, :, :, :, part].reshape(side, 16, size), me_x
        total = own.astype(F32)
        for k in range(1, side):
            if axis == "x":
                total = total + line_recv_x[k - 1, :, :, part].astype(F32)
            else:
                total = total + line_recv[k - 1, :, :, :, part].astype(F32).reshape(side, 16, size)
        line_sum[:, :, part] = total.astype(BF16)
        crossing[p] = [
            line_copy(
                2 + p,
                k,
                "y" if axis == "x" else "x",
                line_sum.at[lax.rem(here + k, side), :, part],
                cross_recv.at[k - 1, :, part],
            )
            for k in range(1, side)
        ]
    total = kvp_reduce(4, send_sq[me_m, me_c], recv_sq)
    inverse = lax.rsqrt(jnp.sum(total[:8], axis=1, keepdims=True) / width + EPSILON)
    base = 5 + len(pieces)
    for p, (at, size, axis) in enumerate(pieces):
        part = pl.ds(at, size)
        if axis is None:
            own = send4[me_y, me_x // 2, me_c, :, part]
            total = kvp_reduce(5 + p, own, recv4.at[:, :, part])
        else:
            for copy in crossing[p]:
                copy.wait_recv()
            total = line_sum[me_y if axis == "x" else me_x, :, part].astype(F32)
            for k in range(1, side):
                total = total + cross_recv[k - 1, :, part].astype(F32)
        gate = total[:8] * inverse
        up = total[8:] * inverse
        middle = gate / (1.0 + jnp.exp(-gate)) * up
        mine = gath4.at[me_m, me_c, :, pl.ds(at // 2, size // 2)]
        mine[...] = folded(middle).astype(BF16)
        kvp_gather(base + p, mine)
    finish()
    arrive(5)
    down_part = jnp.zeros((rows, db), F32)
    for p, (at, size, _) in enumerate(pieces):
        part = pl.ds(at // 2, size // 2)
        kvp_gather_wait(base + p, lambda source, part=part: gath4.at[source // 2, source % 2, :, part])
        for c in range(2):
            rows_of = [gath4[m, c, :, part].astype(F32) for m in range(nm)]
            piece = jnp.concatenate(
                [jnp.concatenate([r[:8] for r in rows_of], axis=0), jnp.concatenate([r[8:] for r in rows_of], axis=0)],
                axis=1,
            ).astype(BF16)
            down_part += dot(piece, wd[c * fh + at : c * fh + at + size, :])
    down = head_sum(nz + 1, down_part, core5, along5)
    final[core] = (resid[core].astype(F32) + down).astype(BF16)
    share_half(2 * nz + 1, final)
    next_ref[:, :half] = final[0]
    next_ref[:, half:] = final[1]
    finish()


def body(
    nk,
    nh,
    hidden_in,
    norm_gain,
    w_query,
    w_key,
    w_value,
    w_out,
    post_gain,
    w_gate,
    w_up,
    w_down,
    cache_keys,
    cache_values,
    context_len,
    slot_request,
    slot_start,
):
    rows, db = hidden_in.shape
    nm = nk // 2
    slots = cache_keys.shape[0]
    fh = w_gate.shape[1] // 2
    half, nz, side, count = db // 2, nh // 2, math.isqrt(nk), len(pieces_of(fh))
    exponent = np.arange(HD // 2, dtype=np.float32) * np.float32(2.0 / HD)
    frequency = (THETA_BASE ** (-exponent.astype(np.float64))).astype(np.float32)
    frequency = jnp.asarray(np.concatenate([frequency, frequency])[None, :])
    vmem = pl.BlockSpec(memory_space=pltpu.VMEM)
    hbm = pl.BlockSpec(memory_space=pl.ANY)
    smem = pl.BlockSpec(memory_space=pltpu.SMEM)
    scratch = [
        pltpu.VMEM(w.shape, BF16)
        for w in (w_query, w_key, w_value, w_out, w_gate, w_up, w_down, cache_keys, cache_values)
    ]
    scratch += [
        pltpu.VMEM((2, rows, half), F32),
        pltpu.VMEM((nm, 2, 16, 384), BF16),
        pltpu.VMEM((nk - 1, 16, 384), BF16),
        pltpu.VMEM((nk, 2, 16, HD), BF16),
        pltpu.VMEM((nm, 2, 16, HD), BF16),
        pltpu.VMEM((slots // 2, HD, 2 * BLOCK), BF16),
        pltpu.VMEM((slots, 32, BLOCK), F32),
        pltpu.VMEM((slots, 32, BLOCK), F32),
        pltpu.VMEM((nk, 32, BLOCK), F32),
        pltpu.VMEM((slots, 32, HD), F32),
        pltpu.VMEM((slots, 32, BLOCK), F32),
        pltpu.VMEM((nm, 2, 48, HD), BF16),
        pltpu.VMEM((nk - 1, 48, HD), BF16),
        pltpu.VMEM((nm, 2, 16, 256), BF16),
        pltpu.VMEM((2, rows, half), BF16),
        pltpu.VMEM((nz, rows, half), BF16),
        pltpu.VMEM((2, rows, half), BF16),
        pltpu.VMEM((nm, 2, 16, HD), BF16),
        pltpu.VMEM((nk - 1, 16, HD), BF16),
        pltpu.VMEM((side, side // 2, 2, 16, fh), BF16),
        pltpu.VMEM((nk - 1, 16, fh), BF16),
        pltpu.VMEM((side - 1, side, 16, fh), BF16),
        pltpu.VMEM((side - 1, side // 2, 2, 16, fh), BF16),
        pltpu.VMEM((side, 16, fh), BF16),
        pltpu.VMEM((side - 1, 16, fh), BF16),
        pltpu.VMEM((nm, 2, 16, fh // 2), BF16),
        pltpu.VMEM((2, rows, half), BF16),
        pltpu.VMEM((nz, rows, half), BF16),
        pltpu.VMEM((2, rows, half), BF16),
        pltpu.SemaphoreType.DMA((9,)),
        pltpu.SemaphoreType.DMA((6 + 2 * count, nk)),
        pltpu.SemaphoreType.DMA((6 + 2 * count, nk)),
        pltpu.SemaphoreType.DMA((2 * nz + 2,)),
        pltpu.SemaphoreType.DMA((2 * nz + 2,)),
        pltpu.SemaphoreType.DMA((4, side)),
        pltpu.SemaphoreType.DMA((4, side)),
    ]
    weight_items = sum(w.size for w in (w_query, w_key, w_value, w_out, w_gate, w_up, w_down))
    results = pl.pallas_call(
        functools.partial(kernel, nk, nh, db * nk),
        out_shape=(
            jax.ShapeDtypeStruct((rows, db), BF16),
            jax.ShapeDtypeStruct((rows, HD), BF16),
            jax.ShapeDtypeStruct((rows, HD), BF16),
        ),
        in_specs=[vmem] * 4 + [hbm] * 9 + [smem] * 3,
        out_specs=(vmem, vmem, vmem),
        scratch_shapes=scratch,
        compiler_params=pltpu.CompilerParams(
            collective_id=0, has_side_effects=True, vmem_limit_bytes=56 * 1024 * 1024
        ),
        cost_estimate=pl.CostEstimate(
            flops=2 * rows * weight_items + 4 * slots * 32 * BLOCK * HD,
            bytes_accessed=2 * (weight_items + 2 * cache_keys.size),
            transcendentals=slots * 32 * BLOCK,
        ),
    )(
        hidden_in,
        norm_gain,
        post_gain,
        frequency,
        w_query,
        w_key,
        w_value,
        w_out,
        w_gate,
        w_up,
        w_down,
        cache_keys,
        cache_values,
        context_len,
        slot_request,
        slot_start,
    )
    return pl.pallas_call(
        hand_on,
        out_shape=tuple(jax.ShapeDtypeStruct(r.shape, r.dtype) for r in results),
        in_specs=[vmem] * 3,
        out_specs=(vmem,) * 3,
    )(*results)


def solution(mesh):
    return jax.shard_map(
        functools.partial(body, mesh.shape["kvp"], mesh.shape["head"]),
        mesh=mesh,
        in_specs=(
            P(None, "kvp"),
            P("kvp"),
            P("kvp", "head"),
            P("kvp", "head"),
            P("kvp", "head"),
            P("head", "kvp"),
            P("kvp"),
            P("kvp", "head"),
            P("kvp", "head"),
            P("head", "kvp"),
            P("kvp", None, "head"),
            P("kvp", None, "head"),
            P(),
            P("kvp"),
            P("kvp"),
        ),
        out_specs=(P(None, "kvp"), P(None, "head"), P(None, "head")),
        check_vma=False,
    )
```

```python
import functools
import math

import jax
import jax.numpy as jnp
import numpy as np
from jax import lax
from jax.experimental import pallas as pl
from jax.experimental.pallas import tpu as pltpu
from jax.sharding import PartitionSpec as P

HD = 128
DRAFT = 4
BLOCK = 128
EPSILON = 1e-05
THETA_BASE = 500000.0
FLOOR = -1e30
LOG2E = math.log2(math.e)
EXP_SCALE = LOG2E / math.sqrt(HD)
UNROLL = 80
MESH = pl.DeviceIdType.MESH
F32 = jnp.float32
BF16 = jnp.bfloat16


def iota(shape, dim):
    return lax.broadcasted_iota(jnp.int32, shape, dim)


def dot(a, b):
    return jnp.dot(a, b, preferred_element_type=F32)


def dot_t(a, b):
    return lax.dot_general(a, b, (((1,), (1,)), ((), ())), preferred_element_type=F32)


def three_parts(x):
    high = x.astype(BF16).astype(F32)
    middle = (x - high).astype(BF16).astype(F32)
    return high, middle, x - high - middle


def pieces_of(columns):
    size = max(256, columns * 3 // 7 // 256 * 256)
    return [(0, size, "x"), (size, size, "y"), (2 * size, columns - 2 * size, None)]


def hand_on(a_ref, b_ref, c_ref, a_out, b_out, c_out):
    a_out[...] = a_ref[...]
    b_out[...] = b_ref[...]
    c_out[...] = c_ref[...]


def kernel(
    nk,
    nh,
    width,
    hid_hbm,
    gain_hbm,
    post_hbm,
    freq_hbm,
    wq_hbm,
    wk_hbm,
    wv_hbm,
    wo_hbm,
    wg_hbm,
    wu_hbm,
    wd_hbm,
    keys_hbm,
    values_hbm,
    ctx_hbm,
    req_hbm,
    start_hbm,
    next_ref,
    dkey_ref,
    dval_ref,
    hid_ref,
    gain_ref,
    post_ref,
    freq_ref,
    ctx_ref,
    req_ref,
    start_ref,
    wq,
    wk,
    wv,
    wo,
    wg,
    wu,
    wd,
    keys,
    values,
    hidden_halves,
    send1,
    recv1,
    gath1,
    draft_kv,
    turned_keys,
    scores,
    runs,
    tops,
    outs,
    sums,
    send2,
    recv2,
    gath2,
    core3,
    along3,
    resid,
    send_sq,
    recv_sq,
    send4,
    recv4,
    line_recv_x,
    line_recv,
    line_sum,
    cross_recv,
    gath4,
    core5,
    along5,
    final,
    local_sem,
    ksend_sem,
    krecv_sem,
    hsend_sem,
    hrecv_sem,
    lsend_sem,
    lrecv_sem,
):
    me_k = lax.axis_index("kvp")
    me_h = lax.axis_index("head")
    nm = nk // 2
    nz = nh // 2
    me_z, core = me_h // 2, me_h % 2
    twin = me_h + 1 - 2 * core

    def along_z(k):
        return lax.rem(me_z + k, nz) * 2 + core

    rows = 8 * nm
    me_m, me_c = me_k // 2, me_k % 2
    side = math.isqrt(nk)
    me_y, me_x = me_k // side, me_k % side
    slots = keys.shape[0]
    db = hid_ref.shape[1]
    half = db // 2
    ff = wg.shape[1]
    fh = ff // 2
    pieces = pieces_of(fh)

    sent = []

    offsets = [(dy, dx) for dy in range(side) for dx in range(side) if dy or dx]
    offsets.sort(key=lambda o: -sum(min(d, side - d) for d in o))
    targets = [
        lax.rem(me_y + dy, side) * side + lax.rem(me_x + dx, side) for dy, dx in offsets
    ]
    sources = [
        lax.rem(me_y + side - dy, side) * side + lax.rem(me_x + side - dx, side) for dy, dx in offsets
    ]
    near_first = list(reversed(range(nk - 1)))
    barrier = pltpu.get_barrier_semaphore()
    for to in targets:
        pl.semaphore_signal(barrier, inc=1, device_id=(to, me_h), device_id_type=MESH)
    for to in [twin] + [along_z(k) for k in range(1, nz)]:
        pl.semaphore_signal(barrier, inc=1, device_id=(me_k, to), device_id_type=MESH)

    first_copies = [
        pltpu.make_async_copy(src, dst, local_sem.at[i])
        for i, (src, dst) in enumerate([(wq_hbm, wq), (wk_hbm, wk), (wv_hbm, wv)])
    ]
    small_copies = [
        pltpu.make_async_copy(src, dst, local_sem.at[9 + i])
        for i, (src, dst) in enumerate(
            [
                (hid_hbm, hid_ref),
                (gain_hbm, gain_ref),
                (post_hbm, post_ref),
                (freq_hbm, freq_ref),
                (ctx_hbm, ctx_ref),
                (req_hbm, req_ref),
                (start_hbm, start_ref),
            ]
        )
    ]
    later_copies = [
        pltpu.make_async_copy(src, dst, local_sem.at[3 + i])
        for i, (src, dst) in enumerate(
            [(keys_hbm, keys), (values_hbm, values), (wo_hbm, wo), (wg_hbm, wg), (wu_hbm, wu), (wd_hbm, wd)]
        )
    ]
    def arrive(i):
        later_copies[i].wait()

    for c in small_copies + first_copies:
        c.start()


    def kvp_copy(phase, i, src, dst):
        return pltpu.make_async_remote_copy(
            src_ref=src,
            dst_ref=dst,
            send_sem=ksend_sem.at[phase, i],
            recv_sem=krecv_sem.at[phase, i],
            device_id=(targets[i], me_h),
            device_id_type=MESH,
        )

    def kvp_start(phase, i, src, dst):
        copy = kvp_copy(phase, i, src, dst)
        copy.start()
        sent.append(copy)

    def head_copy(sem, to, src, dst):
        return pltpu.make_async_remote_copy(
            src_ref=src,
            dst_ref=dst,
            send_sem=hsend_sem.at[sem],
            recv_sem=hrecv_sem.at[sem],
            device_id=(me_k, to),
            device_id_type=MESH,
        )

    def line_copy(sem, k, axis, src, dst):
        if axis == "x":
            to = me_y * side + lax.rem(me_x + k, side)
        else:
            to = lax.rem(me_y + k, side) * side + me_x
        copy = pltpu.make_async_remote_copy(
            src_ref=src,
            dst_ref=dst,
            send_sem=lsend_sem.at[sem, k],
            recv_sem=lrecv_sem.at[sem, k],
            device_id=(to, me_h),
            device_id_type=MESH,
        )
        copy.start()
        sent.append(copy)
        return copy

    def kvp_scatter(phase, send, recv):
        for i, to in enumerate(targets):
            kvp_start(phase, i, send.at[to // 2, to % 2], recv.at[i])

    def kvp_gather(phase, mine):
        for i in range(nk - 1):
            kvp_start(phase, i, mine, mine)

    def kvp_await(phase, i, ref):
        kvp_copy(phase, i, ref, ref).wait_recv()

    def kvp_gather_wait(phase, slot):
        for i in near_first:
            kvp_await(phase, i, slot(sources[i]))

    def kvp_reduce(phase, own, recv):
        total = own.astype(F32)
        for i in near_first:
            kvp_await(phase, i, recv.at[i])
            total = total + recv[i].astype(F32)
        return total

    def halves(x):
        return x[:, :half], x[:, half:]

    def head_sum(base, part_of, swap_ref, along_ref):
        swap_ref[0] = part_of(1 - core).astype(BF16)
        swapped = head_copy(base, twin, swap_ref.at[0], swap_ref.at[1])
        swapped.start()
        sent.append(swapped)
        own = part_of(core)
        swapped.wait_recv()
        along_ref[0] = (own + swap_ref[1].astype(F32)).astype(BF16)
        copies = [head_copy(base + k, along_z(k), along_ref.at[0], along_ref.at[k]) for k in range(1, nz)]
        for copy in copies:
            copy.start()
        sent.extend(copies)
        for copy in copies:
            copy.wait_recv()
        total = jnp.zeros((rows, half), F32)
        for z in range(nz):
            total = total + along_ref[lax.rem(me_z - z + nz, nz)].astype(F32)
        return total

    def share_half(sem, ref):
        copy = head_copy(sem, twin, ref.at[core], ref.at[core])
        copy.start()
        sent.append(copy)
        copy.wait_recv()

    def finish():
        while sent:
            sent.pop(0).wait_send()

    def folded(x):
        return jnp.concatenate([x[:, : x.shape[1] // 2], x[:, x.shape[1] // 2 :]], axis=0)

    for c in small_copies:
        c.wait()
    hidden = hid_ref[...].astype(F32)
    hidden_halves[0], hidden_halves[1] = halves(hidden)
    scaled = (hidden * gain_ref[...].astype(F32).reshape(1, db)).astype(BF16)
    square = jnp.sum(hidden * hidden, axis=1, keepdims=True)
    lane = iota((rows, HD), 1)

    def square_tile(column):
        high, middle, low = three_parts(jnp.broadcast_to(column, (rows, HD)))
        return jnp.where(lane == 0, high, jnp.where(lane == 1, middle, jnp.where(lane == 2, low, 0.0)))

    square_in = square_tile(square)
    for c in first_copies:
        c.wait()
    for c in later_copies:
        c.start()
    key_part = dot(scaled, wk[...])
    value_part = dot(scaled, wv[...])
    for c in range(2):
        query_part = dot(scaled, wq[:, c * 512 : (c + 1) * 512])
        upper = query_part[:, :384]
        lower = jnp.concatenate([query_part[:, 384:], value_part if c else key_part, square_in], axis=1)
        send1[:, c] = jnp.concatenate([upper.reshape(nm, 8, 384), lower.reshape(nm, 8, 384)], axis=1).astype(BF16)

    eight = iota((8, HD), 0)
    lane8 = iota((8, HD), 1)
    position = jnp.where(eight < DRAFT, ctx_ref[2 * me_m], ctx_ref[2 * me_m + 1]) + eight % DRAFT
    angle = position.astype(F32) * freq_ref[...]
    cosine = jnp.cos(angle)
    sine = jnp.sin(angle)
    sine = jnp.where(lane8 < HD // 2, -sine, sine)

    def find_last(s, last):
        return jnp.where(lane8 == req_ref[s], s, last)

    last_slots = lax.fori_loop(0, slots, find_last, jnp.full((8, HD), -1, jnp.int32), unroll=8)
    last_of = [jnp.max(jnp.where(lane8 == b, last_slots, -1)) for b in range(nk)]
    pl.semaphore_wait(barrier, nk + nz - 1)
    kvp_scatter(0, send1, recv1)

    arrive(0)

    def turn_keys(i, _):
        for u in range(4):
            n = 4 * i + u
            turned_keys[n, :, :BLOCK] = keys[2 * n].T
            turned_keys[n, :, BLOCK:] = keys[2 * n + 1].T
        return 0

    lax.fori_loop(0, slots // 8, turn_keys, 0)
    total = kvp_reduce(0, send1[me_m, me_c], recv1)
    square_sum = jnp.sum(total[8:, 256:], axis=1, keepdims=True)
    inverse = lax.rsqrt(square_sum / width + EPSILON)
    tiles = [total[:8, :128], total[:8, 128:256], total[:8, 256:], total[8:, :128], total[8:, 128:256]]
    tiles = [t * inverse for t in tiles]
    rotated = [t * cosine + pltpu.roll(t, HD // 2, 1) * sine for t in tiles]
    low_rows = eight < DRAFT

    def swap(x):
        return pltpu.roll(x, DRAFT, 0)

    def first_of(a, b):
        return jnp.where(low_rows, a, swap(b))

    def second_of(a, b):
        return jnp.where(low_rows, swap(a), b)

    q0, q1, q2, q3 = rotated[:4]
    pair = jnp.where(me_c == 0, rotated[4], tiles[4])
    query_slot = gath1.at[pl.ds(2 * me_m, 2), me_c]
    query_slot[0] = jnp.concatenate([first_of(q0, q1), first_of(q2, q3)], axis=0).astype(BF16)
    query_slot[1] = jnp.concatenate([second_of(q0, q1), second_of(q2, q3)], axis=0).astype(BF16)
    draft_kv[me_m, me_c] = jnp.concatenate([pair, jnp.zeros_like(pair)], axis=0).astype(BF16)
    kvp_gather(1, query_slot)
    kv_phase = 5 + 2 * len(pieces)
    kvp_gather(kv_phase, draft_kv.at[me_m, me_c])
    kvp_gather_wait(1, lambda source: gath1.at[pl.ds(2 * (source // 2), 2), source % 2])
    token = iota((32, BLOCK), 1)

    def previous(s):
        return req_ref[jnp.maximum(s - 1, 0)]

    def score_step(i, run):
        for u in range(0, UNROLL, 2):
            s = i * UNROLL + u
            request = [req_ref[s], req_ref[s + 1]]
            safe = [jnp.maximum(r, 0) for r in request]
            both = jnp.concatenate([gath1[r].reshape(32, HD) for r in safe], axis=0)
            product = dot(both, turned_keys[i * (UNROLL // 2) + u // 2])
            for v in range(2):
                r = request[v]
                live = jnp.where(r >= 0, ctx_ref[safe[v]] - start_ref[s + v], 0)
                part = product[32 * v : 32 * v + 32, BLOCK * v : BLOCK * v + BLOCK]
                part = jnp.where(token < live, part, FLOOR)
                scores[s + v] = part
                run = jnp.maximum(part, jnp.where(r == previous(s + v), run, FLOOR))
                runs[s + v] = run
        return run

    floor_tile = jnp.full((32, BLOCK), FLOOR, F32)
    lax.fori_loop(0, slots // UNROLL, score_step, floor_tile)
    for b in range(nk):
        run = runs[jnp.maximum(last_of[b], 0)]
        top = jnp.max(run, axis=1, keepdims=True)
        tops[b] = jnp.where(last_of[b] >= 0, jnp.broadcast_to(top, (32, BLOCK)), FLOOR)

    arrive(1)

    def value_step(i, carry):
        sum_run, out_run = carry
        for u in range(0, UNROLL, 2):
            s = i * UNROLL + u
            weight = [
                jnp.exp2((scores[s + v] - tops[jnp.maximum(req_ref[s + v], 0)]) * EXP_SCALE) for v in range(2)
            ]
            product = dot(
                jnp.concatenate(weight, axis=0).astype(BF16), jnp.concatenate([values[s], values[s + 1]], axis=1)
            )
            for v in range(2):
                keep = jnp.where(req_ref[s + v] == previous(s + v), 1.0, 0.0).astype(F32)
                sum_run = sum_run * keep + weight[v]
                out_run = out_run * keep + product[32 * v : 32 * v + 32, HD * v : HD * v + HD]
                sums[s + v] = sum_run
                outs[s + v] = out_run
        return sum_run, out_run

    zero_tile = jnp.zeros((32, BLOCK), F32)
    lax.fori_loop(0, slots // UNROLL, value_step, (zero_tile, zero_tile))

    lane32 = iota((32, HD), 1)
    stats = zero_tile
    totals = []
    for b in range(nk):
        at = jnp.maximum(last_of[b], 0)
        here = last_of[b] >= 0
        out = jnp.where(here, outs[at], 0.0)
        column = jnp.sum(sums[at], axis=1, keepdims=True)
        totals.append(jnp.where(here, jnp.broadcast_to(column, (32, HD)), 0.0))
        for c in range(2):
            send2[b // 2, c, 16 * (b % 2) : 16 * (b % 2) + 16, :] = out[16 * c : 16 * c + 16].astype(BF16)
    for m in range(nm):
        for c in range(2):
            j = 2 * m + c
            part = slice(16 * c, 16 * c + 16)
            top = jnp.concatenate([tops[2 * m, part], tops[2 * m + 1, part]], axis=0)
            summed = jnp.concatenate([totals[2 * m][part], totals[2 * m + 1][part]], axis=0)
            stats = jnp.where(lane32 // 8 == j, jnp.where(lane32 % 8 < 3, top, summed), stats)
    high, middle, low = three_parts(stats)
    kind = lane32 % 8
    stats = jnp.where(
        kind % 3 == 0, high, jnp.where(kind % 3 == 1, middle, low)
    )
    stats = jnp.where(kind < 6, stats, 0.0)
    turned = jnp.concatenate([stats, jnp.zeros((HD - 32, HD), F32)], axis=0).T
    for m in range(nm):
        for c in range(2):
            j = 2 * m + c
            tile = jnp.concatenate([turned[8 * j : 8 * j + 8], jnp.zeros((8, HD), F32)], axis=0)
            send2[m, c, 32:48, :] = tile.astype(BF16)
    kvp_scatter(2, send2, recv2)

    finish()
    kvp_gather_wait(kv_phase, lambda source: draft_kv.at[source // 2, source % 2])
    for c, out_ref in enumerate((dkey_ref, dval_ref)):
        out_ref[...] = jnp.concatenate([draft_kv[m, c].astype(F32)[:8] for m in range(nm)], axis=0).astype(BF16)
    mine = gath1[pl.ds(2 * me_m, 2), me_c].reshape(32, HD)
    draft_score = dot_t(mine, draft_kv[me_m, 0])
    row16, col16 = iota((32, 16), 0), iota((32, 16), 1)
    seen = (col16 // DRAFT == row16 // 16) & (col16 % DRAFT <= row16 % DRAFT)
    draft_score = jnp.where(seen, draft_score, FLOOR)
    draft_top = jnp.max(draft_score, axis=1, keepdims=True)
    draft_weight = jnp.where(seen, jnp.exp2((draft_score - draft_top) * EXP_SCALE), 0.0)
    draft_sum = jnp.sum(draft_weight, axis=1, keepdims=True)
    draft_out = dot(draft_weight.astype(BF16), draft_kv[me_m, 1])

    for i in near_first:
        kvp_await(2, i, recv2.at[i])
    partials = [send2.at[me_m, me_c]] + [recv2.at[i] for i in range(nk - 1)]
    every = [p[32:48, :].astype(F32)[:8] for p in partials]
    every = jnp.concatenate(every + [jnp.zeros((8, HD), F32)] * (HD // 8 - nk), axis=0)
    turned = every.T[:32]
    joined = turned + pltpu.roll(turned, HD - 1, 1) + pltpu.roll(turned, HD - 2, 1)
    own_lane = (lane32 % 8 == 0) & (lane32 < 8 * nk)
    peak = jnp.max(jnp.where(own_lane, joined, FLOOR), axis=1, keepdims=True)
    peak = jnp.maximum(peak, draft_top)
    factor = jnp.where(own_lane, jnp.exp2((joined - peak) * EXP_SCALE), 0.0)
    whole = jnp.where(own_lane, factor * pltpu.roll(joined, HD - 3, 1), 0.0)
    draft_factor = jnp.exp2((draft_top - peak) * EXP_SCALE)
    whole = jnp.sum(whole, axis=1, keepdims=True) + draft_sum * draft_factor
    factor = factor / whole
    mixed = draft_out * (draft_factor / whole)
    for i in range(nk):
        mixed = mixed + partials[i][:32, :].astype(F32) * factor[:, 8 * i : 8 * i + 1]
    a0, a1, b0, b1 = mixed[:8], mixed[8:16], mixed[16:24], mixed[24:]
    h0, h1 = first_of(a0, b0), second_of(a0, b0)
    h2, h3 = first_of(a1, b1), second_of(a1, b1)
    gath2[me_m, me_c] = jnp.concatenate(
        [jnp.concatenate([h0, h1], axis=1), jnp.concatenate([h2, h3], axis=1)], axis=0
    ).astype(BF16)
    kvp_gather(3, gath2.at[me_m, me_c])
    finish()
    arrive(2)
    kvp_gather_wait(3, lambda source: gath2.at[source // 2, source % 2])

    heads = [
        jnp.concatenate([gath2[m, c].astype(F32)[8 * g : 8 * g + 8] for m in range(nm)], axis=0).astype(BF16)
        for c in range(2)
        for g in range(2)
    ]

    def attn_half(which):
        columns = pl.ds(pl.multiple_of(which * half, half), half)
        return sum(dot(heads[n], wo[256 * n : 256 * n + 256, columns]) for n in range(4))

    attn = head_sum(0, attn_half, core3, along3)
    resid[core] = (hidden_halves[core] + attn).astype(BF16)
    share_half(nz, resid)
    residual = jnp.concatenate([resid[0].astype(F32), resid[1].astype(F32)], axis=1)
    normed = (residual * post_ref[...].astype(F32).reshape(1, db)).astype(BF16)
    arrive(3)
    arrive(4)
    lines, direct = {}, []
    for p, (at, size, axis) in enumerate(pieces):
        part = pl.ds(at, size)
        for c in range(2):
            columns = slice(c * fh + at, c * fh + at + size)
            gate = dot(normed, wg[:, columns]).reshape(nm, 8, size)
            up = dot(normed, wu[:, columns]).reshape(nm, 8, size)
            both = jnp.concatenate([gate, up], axis=1).astype(BF16)
            send4[:, :, c, :, part] = both.reshape(side, side // 2, 16, size)
        if axis is None:
            direct.append((p, part))
            continue
        lines[p] = []
        for k in [side // 2] + [k for k in range(1, side) if k != side // 2]:
            if axis == "x":
                x = lax.rem(me_x + k, side)
                src, dst = send4.at[:, x // 2, x % 2, :, part], line_recv_x.at[k - 1, :, :, part]
            else:
                y = lax.rem(me_y + k, side)
                src, dst = send4.at[y, :, :, :, part], line_recv.at[k - 1, :, :, :, part]
            lines[p].append(line_copy(p, k, axis, src, dst))
        if p == 0:
            square_out = square_tile(jnp.sum(residual * residual, axis=1, keepdims=True)).reshape(nm, 8, HD)
            square_out = jnp.concatenate([square_out, jnp.zeros_like(square_out)], axis=1).astype(BF16)
            send_sq[:, 0] = square_out
            send_sq[:, 1] = square_out
            kvp_scatter(4, send_sq, recv_sq)
    for p, part in direct:
        for i, to in enumerate(targets):
            src = send4.at[to // side, (to % side) // 2, to % 2, :, part]
            kvp_start(5 + p, i, src, recv4.at[i, :, part])
    crossing = {}
    for p, (at, size, axis) in enumerate(pieces):
        if axis is None:
            continue
        part = pl.ds(at, size)
        for copy in lines[p]:
            copy.wait_recv()
        if axis == "x":
            own, here = send4[:, me_x // 2, me_x % 2, :, part], me_y
        else:
            own, here = send4[me_y, :, :, :, part].reshape(side, 16, size), me_x
        total = own.astype(F32)
        for k in range(1, side):
            if axis == "x":
                total = total + line_recv_x[k - 1, :, :, part].astype(F32)
            else:
                total = total + line_recv[k - 1, :, :, :, part].astype(F32).reshape(side, 16, size)
        line_sum[:, :, part] = total.astype(BF16)
        crossing[p] = [
            line_copy(
                2 + p,
                k,
                "y" if axis == "x" else "x",
                line_sum.at[lax.rem(here + k, side), :, part],
                cross_recv.at[k - 1, :, part],
            )
            for k in range(1, side)
        ]
    total = kvp_reduce(4, send_sq[me_m, me_c], recv_sq)
    inverse = lax.rsqrt(jnp.sum(total[:8], axis=1, keepdims=True) / width + EPSILON)
    base = 5 + len(pieces)
    order = [2, 0, 1]
    for p, (at, size, axis) in [(p, pieces[p]) for p in order]:
        part = pl.ds(at, size)
        if axis is None:
            own = send4[me_y, me_x // 2, me_c, :, part]
            total = kvp_reduce(5 + p, own, recv4.at[:, :, part])
        else:
            for copy in crossing[p]:
                copy.wait_recv()
            total = line_sum[me_y if axis == "x" else me_x, :, part].astype(F32)
            for k in range(1, side):
                total = total + cross_recv[k - 1, :, part].astype(F32)
        gate = total[:8] * inverse
        up = total[8:] * inverse
        middle = gate / (1.0 + jnp.exp(-gate)) * up
        mine = gath4.at[me_m, me_c, :, pl.ds(at // 2, size // 2)]
        mine[...] = folded(middle).astype(BF16)
        kvp_gather(base + p, mine)
    finish()
    arrive(5)
    down_part = jnp.zeros((rows, db), F32)
    for p, (at, size, _) in [(p, pieces[p]) for p in order]:
        part = pl.ds(at // 2, size // 2)
        kvp_gather_wait(base + p, lambda source, part=part: gath4.at[source // 2, source % 2, :, part])
        for c in range(2):
            rows_of = [gath4[m, c, :, part].astype(F32) for m in range(nm)]
            piece = jnp.concatenate(
                [jnp.concatenate([r[:8] for r in rows_of], axis=0), jnp.concatenate([r[8:] for r in rows_of], axis=0)],
                axis=1,
            ).astype(BF16)
            down_part += dot(piece, wd[c * fh + at : c * fh + at + size, :])
    down = head_sum(nz + 1, lambda which: jnp.where(which == 0, *halves(down_part)), core5, along5)
    final[core] = (resid[core].astype(F32) + down).astype(BF16)
    share_half(2 * nz + 1, final)
    next_ref[:, :half] = final[0]
    next_ref[:, half:] = final[1]
    finish()


def body(
    nk,
    nh,
    hidden_in,
    norm_gain,
    w_query,
    w_key,
    w_value,
    w_out,
    post_gain,
    w_gate,
    w_up,
    w_down,
    cache_keys,
    cache_values,
    context_len,
    slot_request,
    slot_start,
):
    rows, db = hidden_in.shape
    nm = nk // 2
    slots = cache_keys.shape[0]
    fh = w_gate.shape[1] // 2
    half, nz, side, count = db // 2, nh // 2, math.isqrt(nk), len(pieces_of(fh))
    exponent = np.arange(HD // 2, dtype=np.float32) * np.float32(2.0 / HD)
    frequency = (THETA_BASE ** (-exponent.astype(np.float64))).astype(np.float32)
    frequency = jnp.asarray(np.concatenate([frequency, frequency])[None, :])
    vmem = pl.BlockSpec(memory_space=pltpu.VMEM)
    hbm = pl.BlockSpec(memory_space=pl.ANY)
    scratch = [
        pltpu.VMEM(hidden_in.shape, BF16),
        pltpu.VMEM(norm_gain.shape, BF16),
        pltpu.VMEM(post_gain.shape, BF16),
        pltpu.VMEM(frequency.shape, F32),
        pltpu.SMEM(context_len.shape, jnp.int32),
        pltpu.SMEM(slot_request.shape, jnp.int32),
        pltpu.SMEM(slot_start.shape, jnp.int32),
    ]
    scratch += [
        pltpu.VMEM(w.shape, BF16)
        for w in (w_query, w_key, w_value, w_out, w_gate, w_up, w_down, cache_keys, cache_values)
    ]
    scratch += [
        pltpu.VMEM((2, rows, half), F32),
        pltpu.VMEM((nm, 2, 16, 384), BF16),
        pltpu.VMEM((nk - 1, 16, 384), BF16),
        pltpu.VMEM((nk, 2, 16, HD), BF16),
        pltpu.VMEM((nm, 2, 16, HD), BF16),
        pltpu.VMEM((slots // 2, HD, 2 * BLOCK), BF16),
        pltpu.VMEM((slots, 32, BLOCK), F32),
        pltpu.VMEM((slots, 32, BLOCK), F32),
        pltpu.VMEM((nk, 32, BLOCK), F32),
        pltpu.VMEM((slots, 32, HD), F32),
        pltpu.VMEM((slots, 32, BLOCK), F32),
        pltpu.VMEM((nm, 2, 48, HD), BF16),
        pltpu.VMEM((nk - 1, 48, HD), BF16),
        pltpu.VMEM((nm, 2, 16, 256), BF16),
        pltpu.VMEM((2, rows, half), BF16),
        pltpu.VMEM((nz, rows, half), BF16),
        pltpu.VMEM((2, rows, half), BF16),
        pltpu.VMEM((nm, 2, 16, HD), BF16),
        pltpu.VMEM((nk - 1, 16, HD), BF16),
        pltpu.VMEM((side, side // 2, 2, 16, fh), BF16),
        pltpu.VMEM((nk - 1, 16, fh), BF16),
        pltpu.VMEM((side - 1, side, 16, fh), BF16),
        pltpu.VMEM((side - 1, side // 2, 2, 16, fh), BF16),
        pltpu.VMEM((side, 16, fh), BF16),
        pltpu.VMEM((side - 1, 16, fh), BF16),
        pltpu.VMEM((nm, 2, 16, fh // 2), BF16),
        pltpu.VMEM((2, rows, half), BF16),
        pltpu.VMEM((nz, rows, half), BF16),
        pltpu.VMEM((2, rows, half), BF16),
        pltpu.SemaphoreType.DMA((16,)),
        pltpu.SemaphoreType.DMA((6 + 2 * count, nk)),
        pltpu.SemaphoreType.DMA((6 + 2 * count, nk)),
        pltpu.SemaphoreType.DMA((2 * nz + 2,)),
        pltpu.SemaphoreType.DMA((2 * nz + 2,)),
        pltpu.SemaphoreType.DMA((4, side)),
        pltpu.SemaphoreType.DMA((4, side)),
    ]
    weight_items = sum(w.size for w in (w_query, w_key, w_value, w_out, w_gate, w_up, w_down))
    results = pl.pallas_call(
        functools.partial(kernel, nk, nh, db * nk),
        out_shape=(
            jax.ShapeDtypeStruct((rows, db), BF16),
            jax.ShapeDtypeStruct((rows, HD), BF16),
            jax.ShapeDtypeStruct((rows, HD), BF16),
        ),
        in_specs=[hbm] * 16,
        out_specs=(vmem, vmem, vmem),
        scratch_shapes=scratch,
        compiler_params=pltpu.CompilerParams(
            collective_id=0, has_side_effects=True, vmem_limit_bytes=56 * 1024 * 1024
        ),
        cost_estimate=pl.CostEstimate(
            flops=2 * rows * weight_items + 4 * slots * 32 * BLOCK * HD,
            bytes_accessed=2 * (weight_items + 2 * cache_keys.size),
            transcendentals=slots * 32 * BLOCK,
        ),
    )(
        hidden_in,
        norm_gain,
        post_gain,
        frequency,
        w_query,
        w_key,
        w_value,
        w_out,
        w_gate,
        w_up,
        w_down,
        cache_keys,
        cache_values,
        context_len,
        slot_request,
        slot_start,
    )
    return pl.pallas_call(
        hand_on,
        out_shape=tuple(jax.ShapeDtypeStruct(r.shape, r.dtype) for r in results),
        in_specs=[vmem] * 3,
        out_specs=(vmem,) * 3,
    )(*results)


def solution(mesh):
    return jax.shard_map(
        functools.partial(body, mesh.shape["kvp"], mesh.shape["head"]),
        mesh=mesh,
        in_specs=(
            P(None, "kvp"),
            P("kvp"),
            P("kvp", "head"),
            P("kvp", "head"),
            P("kvp", "head"),
            P("head", "kvp"),
            P("kvp"),
            P("kvp", "head"),
            P("kvp", "head"),
            P("head", "kvp"),
            P("kvp", None, "head"),
            P("kvp", None, "head"),
            P(),
            P("kvp"),
            P("kvp"),
        ),
        out_specs=(P(None, "kvp"), P(None, "head"), P(None, "head")),
        check_vma=False,
    )
```

```python
import functools
import math

import jax
import jax.numpy as jnp
import numpy as np
from jax import lax
from jax.experimental import pallas as pl
from jax.experimental.pallas import tpu as pltpu
from jax.sharding import PartitionSpec as P

HD = 128
DRAFT = 4
BLOCK = 128
EPSILON = 1e-05
THETA_BASE = 500000.0
FLOOR = -1e30
LOG2E = math.log2(math.e)
EXP_SCALE = LOG2E / math.sqrt(HD)
UNROLL = 160
MESH = pl.DeviceIdType.MESH
F32 = jnp.float32
BF16 = jnp.bfloat16


def iota(shape, dim):
    return lax.broadcasted_iota(jnp.int32, shape, dim)


def dot(a, b):
    return jnp.dot(a, b, preferred_element_type=F32)


def dot_t(a, b):
    return lax.dot_general(a, b, (((1,), (1,)), ((), ())), preferred_element_type=F32)


def three_parts(x):
    high = x.astype(BF16).astype(F32)
    middle = (x - high).astype(BF16).astype(F32)
    return high, middle, x - high - middle


def pieces_of(columns):
    size = max(256, columns * 3 // 7 // 256 * 256)
    return [(0, size, "x"), (size, size, "y"), (2 * size, columns - 2 * size, None)]


def hand_on(a_ref, b_ref, c_ref, a_out, b_out, c_out):
    a_out[...] = a_ref[...]
    b_out[...] = b_ref[...]
    c_out[...] = c_ref[...]


def kernel(
    nk,
    nh,
    width,
    hid_hbm,
    gain_hbm,
    post_hbm,
    freq_hbm,
    wq_hbm,
    wk_hbm,
    wv_hbm,
    wo_hbm,
    wg_hbm,
    wu_hbm,
    wd_hbm,
    keys_hbm,
    values_hbm,
    ctx_hbm,
    req_hbm,
    start_hbm,
    next_ref,
    dkey_ref,
    dval_ref,
    hid_ref,
    gain_ref,
    post_ref,
    freq_ref,
    ctx_ref,
    req_ref,
    start_ref,
    wq,
    wk,
    wv,
    wo,
    wg,
    wu,
    wd,
    keys,
    values,
    hidden_halves,
    send1,
    recv1,
    gath1,
    draft_kv,
    turned_keys,
    scores,
    runs,
    tops,
    outs,
    sums,
    send2,
    recv2,
    gath2,
    core3,
    along3,
    resid,
    send_sq,
    recv_sq,
    send4,
    recv4,
    line_recv_x,
    line_recv,
    line_sum,
    cross_recv,
    gath4,
    core5,
    along5,
    final,
    local_sem,
    ksend_sem,
    krecv_sem,
    hsend_sem,
    hrecv_sem,
    lsend_sem,
    lrecv_sem,
):
    me_k = lax.axis_index("kvp")
    me_h = lax.axis_index("head")
    nm = nk // 2
    nz = nh // 2
    me_z, core = me_h // 2, me_h % 2
    twin = me_h + 1 - 2 * core

    def along_z(k):
        return lax.rem(me_z + k, nz) * 2 + core

    rows = 8 * nm
    me_m, me_c = me_k // 2, me_k % 2
    side = math.isqrt(nk)
    me_y, me_x = me_k // side, me_k % side
    slots = keys.shape[0]
    db = hid_ref.shape[1]
    half = db // 2
    ff = wg.shape[1]
    fh = ff // 2
    pieces = pieces_of(fh)

    sent = []

    offsets = [(dy, dx) for dy in range(side) for dx in range(side) if dy or dx]
    offsets.sort(key=lambda o: -sum(min(d, side - d) for d in o))
    targets = [
        lax.rem(me_y + dy, side) * side + lax.rem(me_x + dx, side) for dy, dx in offsets
    ]
    sources = [
        lax.rem(me_y + side - dy, side) * side + lax.rem(me_x + side - dx, side) for dy, dx in offsets
    ]
    near_first = list(reversed(range(nk - 1)))
    barrier = pltpu.get_barrier_semaphore()
    for to in targets:
        pl.semaphore_signal(barrier, inc=1, device_id=(to, me_h), device_id_type=MESH)
    for to in [twin] + [along_z(k) for k in range(1, nz)]:
        pl.semaphore_signal(barrier, inc=1, device_id=(me_k, to), device_id_type=MESH)

    first_copies = [
        pltpu.make_async_copy(src, dst, local_sem.at[i])
        for i, (src, dst) in enumerate([(wq_hbm, wq), (wk_hbm, wk), (wv_hbm, wv)])
    ]
    small_copies = [
        pltpu.make_async_copy(src, dst, local_sem.at[9 + i])
        for i, (src, dst) in enumerate(
            [
                (hid_hbm, hid_ref),
                (gain_hbm, gain_ref),
                (post_hbm, post_ref),
                (freq_hbm, freq_ref),
                (ctx_hbm, ctx_ref),
                (req_hbm, req_ref),
                (start_hbm, start_ref),
            ]
        )
    ]
    later_copies = [
        pltpu.make_async_copy(src, dst, local_sem.at[3 + i])
        for i, (src, dst) in enumerate(
            [(keys_hbm, keys), (values_hbm, values), (wo_hbm, wo), (wg_hbm, wg), (wu_hbm, wu), (wd_hbm, wd)]
        )
    ]
    def arrive(i):
        later_copies[i].wait()

    for c in small_copies + first_copies:
        c.start()


    def kvp_copy(phase, i, src, dst):
        return pltpu.make_async_remote_copy(
            src_ref=src,
            dst_ref=dst,
            send_sem=ksend_sem.at[phase, i],
            recv_sem=krecv_sem.at[phase, i],
            device_id=(targets[i], me_h),
            device_id_type=MESH,
        )

    def kvp_start(phase, i, src, dst):
        copy = kvp_copy(phase, i, src, dst)
        copy.start()
        sent.append(copy)

    def head_copy(sem, to, src, dst):
        return pltpu.make_async_remote_copy(
            src_ref=src,
            dst_ref=dst,
            send_sem=hsend_sem.at[sem],
            recv_sem=hrecv_sem.at[sem],
            device_id=(me_k, to),
            device_id_type=MESH,
        )

    def line_copy(sem, k, axis, src, dst):
        if axis == "x":
            to = me_y * side + lax.rem(me_x + k, side)
        else:
            to = lax.rem(me_y + k, side) * side + me_x
        copy = pltpu.make_async_remote_copy(
            src_ref=src,
            dst_ref=dst,
            send_sem=lsend_sem.at[sem, k],
            recv_sem=lrecv_sem.at[sem, k],
            device_id=(to, me_h),
            device_id_type=MESH,
        )
        copy.start()
        sent.append(copy)
        return copy

    def kvp_scatter(phase, send, recv):
        for i, to in enumerate(targets):
            kvp_start(phase, i, send.at[to // 2, to % 2], recv.at[i])

    def kvp_gather(phase, mine):
        for i in range(nk - 1):
            kvp_start(phase, i, mine, mine)

    def kvp_await(phase, i, ref):
        kvp_copy(phase, i, ref, ref).wait_recv()

    def kvp_gather_wait(phase, slot):
        for i in near_first:
            kvp_await(phase, i, slot(sources[i]))

    def kvp_reduce(phase, own, recv):
        total = own.astype(F32)
        for i in near_first:
            kvp_await(phase, i, recv.at[i])
            total = total + recv[i].astype(F32)
        return total

    def halves(x):
        return x[:, :half], x[:, half:]

    def head_sum(base, part_of, swap_ref, along_ref):
        swap_ref[0] = part_of(1 - core).astype(BF16)
        swapped = head_copy(base, twin, swap_ref.at[0], swap_ref.at[1])
        swapped.start()
        sent.append(swapped)
        own = part_of(core)
        swapped.wait_recv()
        along_ref[0] = (own + swap_ref[1].astype(F32)).astype(BF16)
        copies = [head_copy(base + k, along_z(k), along_ref.at[0], along_ref.at[k]) for k in range(1, nz)]
        for copy in copies:
            copy.start()
        sent.extend(copies)
        for copy in copies:
            copy.wait_recv()
        total = jnp.zeros((rows, half), F32)
        for z in range(nz):
            total = total + along_ref[lax.rem(me_z - z + nz, nz)].astype(F32)
        return total

    def share_half(sem, ref):
        copy = head_copy(sem, twin, ref.at[core], ref.at[core])
        copy.start()
        sent.append(copy)
        copy.wait_recv()

    def finish():
        while sent:
            sent.pop(0).wait_send()

    def folded(x):
        return jnp.concatenate([x[:, : x.shape[1] // 2], x[:, x.shape[1] // 2 :]], axis=0)

    for c in small_copies:
        c.wait()
    hidden = hid_ref[...].astype(F32)
    hidden_halves[0], hidden_halves[1] = halves(hidden)
    scaled = (hidden * gain_ref[...].astype(F32).reshape(1, db)).astype(BF16)
    square = jnp.sum(hidden * hidden, axis=1, keepdims=True)
    lane = iota((rows, HD), 1)

    def square_tile(column):
        high, middle, low = three_parts(jnp.broadcast_to(column, (rows, HD)))
        return jnp.where(lane == 0, high, jnp.where(lane == 1, middle, jnp.where(lane == 2, low, 0.0)))

    square_in = square_tile(square)
    for c in first_copies:
        c.wait()
    for c in later_copies:
        c.start()
    key_part = dot(scaled, wk[...])
    value_part = dot(scaled, wv[...])
    for c in range(2):
        query_part = dot(scaled, wq[:, c * 512 : (c + 1) * 512])
        upper = query_part[:, :384]
        lower = jnp.concatenate([query_part[:, 384:], value_part if c else key_part, square_in], axis=1)
        send1[:, c] = jnp.concatenate([upper.reshape(nm, 8, 384), lower.reshape(nm, 8, 384)], axis=1).astype(BF16)

    eight = iota((8, HD), 0)
    lane8 = iota((8, HD), 1)
    position = jnp.where(eight < DRAFT, ctx_ref[2 * me_m], ctx_ref[2 * me_m + 1]) + eight % DRAFT
    angle = position.astype(F32) * freq_ref[...]
    cosine = jnp.cos(angle)
    sine = jnp.sin(angle)
    sine = jnp.where(lane8 < HD // 2, -sine, sine)

    def find_last(s, last):
        return jnp.where(lane8 == req_ref[s], s, last)

    last_slots = lax.fori_loop(0, slots, find_last, jnp.full((8, HD), -1, jnp.int32), unroll=8)
    last_of = [jnp.max(jnp.where(lane8 == b, last_slots, -1)) for b in range(nk)]
    pl.semaphore_wait(barrier, nk + nz - 1)
    kvp_scatter(0, send1, recv1)

    arrive(0)

    def turn_keys(i, _):
        for u in range(4):
            n = 4 * i + u
            turned_keys[n, :, :BLOCK] = keys[2 * n].T
            turned_keys[n, :, BLOCK:] = keys[2 * n + 1].T
        return 0

    lax.fori_loop(0, slots // 8, turn_keys, 0)
    total = kvp_reduce(0, send1[me_m, me_c], recv1)
    square_sum = jnp.sum(total[8:, 256:], axis=1, keepdims=True)
    inverse = lax.rsqrt(square_sum / width + EPSILON)
    tiles = [total[:8, :128], total[:8, 128:256], total[:8, 256:], total[8:, :128], total[8:, 128:256]]
    tiles = [t * inverse for t in tiles]
    rotated = [t * cosine + pltpu.roll(t, HD // 2, 1) * sine for t in tiles]
    low_rows = eight < DRAFT

    def swap(x):
        return pltpu.roll(x, DRAFT, 0)

    def first_of(a, b):
        return jnp.where(low_rows, a, swap(b))

    def second_of(a, b):
        return jnp.where(low_rows, swap(a), b)

    q0, q1, q2, q3 = rotated[:4]
    pair = jnp.where(me_c == 0, rotated[4], tiles[4])
    query_slot = gath1.at[pl.ds(2 * me_m, 2), me_c]
    query_slot[0] = jnp.concatenate([first_of(q0, q1), first_of(q2, q3)], axis=0).astype(BF16)
    query_slot[1] = jnp.concatenate([second_of(q0, q1), second_of(q2, q3)], axis=0).astype(BF16)
    draft_kv[me_m, me_c] = jnp.concatenate([pair, jnp.zeros_like(pair)], axis=0).astype(BF16)
    kvp_gather(1, query_slot)
    kv_phase = 5 + 2 * len(pieces)
    kvp_gather(kv_phase, draft_kv.at[me_m, me_c])
    kvp_gather_wait(1, lambda source: gath1.at[pl.ds(2 * (source // 2), 2), source % 2])
    token = iota((32, BLOCK), 1)

    def previous(s):
        return req_ref[jnp.maximum(s - 1, 0)]

    def score_step(i, run):
        for u in range(0, UNROLL, 2):
            s = i * UNROLL + u
            request = [req_ref[s], req_ref[s + 1]]
            safe = [jnp.maximum(r, 0) for r in request]
            both = jnp.concatenate([gath1[r].reshape(32, HD) for r in safe], axis=0)
            product = dot(both, turned_keys[i * (UNROLL // 2) + u // 2])
            for v in range(2):
                r = request[v]
                live = jnp.where(r >= 0, ctx_ref[safe[v]] - start_ref[s + v], 0)
                part = product[32 * v : 32 * v + 32, BLOCK * v : BLOCK * v + BLOCK]
                part = jnp.where(token < live, part, FLOOR)
                scores[s + v] = part
                run = jnp.maximum(part, jnp.where(r == previous(s + v), run, FLOOR))
                runs[s + v] = run
        return run

    floor_tile = jnp.full((32, BLOCK), FLOOR, F32)
    lax.fori_loop(0, slots // UNROLL, score_step, floor_tile)
    for b in range(nk):
        run = runs[jnp.maximum(last_of[b], 0)]
        top = jnp.max(run, axis=1, keepdims=True)
        tops[b] = jnp.where(last_of[b] >= 0, jnp.broadcast_to(top, (32, BLOCK)), FLOOR)

    arrive(1)

    def value_step(i, carry):
        sum_run, out_run = carry
        for u in range(0, UNROLL, 2):
            s = i * UNROLL + u
            weight = [
                jnp.exp2((scores[s + v] - tops[jnp.maximum(req_ref[s + v], 0)]) * EXP_SCALE) for v in range(2)
            ]
            product = dot(
                jnp.concatenate(weight, axis=0).astype(BF16), jnp.concatenate([values[s], values[s + 1]], axis=1)
            )
            for v in range(2):
                keep = jnp.where(req_ref[s + v] == previous(s + v), 1.0, 0.0).astype(F32)
                sum_run = sum_run * keep + weight[v]
                out_run = out_run * keep + product[32 * v : 32 * v + 32, HD * v : HD * v + HD]
                sums[s + v] = sum_run
                outs[s + v] = out_run
        return sum_run, out_run

    zero_tile = jnp.zeros((32, BLOCK), F32)
    lax.fori_loop(0, slots // UNROLL, value_step, (zero_tile, zero_tile))

    lane32 = iota((32, HD), 1)
    stats = zero_tile
    totals = []
    for b in range(nk):
        at = jnp.maximum(last_of[b], 0)
        here = last_of[b] >= 0
        out = jnp.where(here, outs[at], 0.0)
        column = jnp.sum(sums[at], axis=1, keepdims=True)
        totals.append(jnp.where(here, jnp.broadcast_to(column, (32, HD)), 0.0))
        for c in range(2):
            send2[b // 2, c, 16 * (b % 2) : 16 * (b % 2) + 16, :] = out[16 * c : 16 * c + 16].astype(BF16)
    for m in range(nm):
        for c in range(2):
            j = 2 * m + c
            part = slice(16 * c, 16 * c + 16)
            top = jnp.concatenate([tops[2 * m, part], tops[2 * m + 1, part]], axis=0)
            summed = jnp.concatenate([totals[2 * m][part], totals[2 * m + 1][part]], axis=0)
            stats = jnp.where(lane32 // 8 == j, jnp.where(lane32 % 8 < 3, top, summed), stats)
    high, middle, low = three_parts(stats)
    kind = lane32 % 8
    stats = jnp.where(
        kind % 3 == 0, high, jnp.where(kind % 3 == 1, middle, low)
    )
    stats = jnp.where(kind < 6, stats, 0.0)
    turned = jnp.concatenate([stats, jnp.zeros((HD - 32, HD), F32)], axis=0).T
    for m in range(nm):
        for c in range(2):
            j = 2 * m + c
            tile = jnp.concatenate([turned[8 * j : 8 * j + 8], jnp.zeros((8, HD), F32)], axis=0)
            send2[m, c, 32:48, :] = tile.astype(BF16)
    kvp_scatter(2, send2, recv2)

    finish()
    kvp_gather_wait(kv_phase, lambda source: draft_kv.at[source // 2, source % 2])
    for c, out_ref in enumerate((dkey_ref, dval_ref)):
        out_ref[...] = jnp.concatenate([draft_kv[m, c].astype(F32)[:8] for m in range(nm)], axis=0).astype(BF16)
    mine = gath1[pl.ds(2 * me_m, 2), me_c].reshape(32, HD)
    draft_score = dot_t(mine, draft_kv[me_m, 0])
    row16, col16 = iota((32, 16), 0), iota((32, 16), 1)
    seen = (col16 // DRAFT == row16 // 16) & (col16 % DRAFT <= row16 % DRAFT)
    draft_score = jnp.where(seen, draft_score, FLOOR)
    draft_top = jnp.max(draft_score, axis=1, keepdims=True)
    draft_weight = jnp.where(seen, jnp.exp2((draft_score - draft_top) * EXP_SCALE), 0.0)
    draft_sum = jnp.sum(draft_weight, axis=1, keepdims=True)
    draft_out = dot(draft_weight.astype(BF16), draft_kv[me_m, 1])

    for i in near_first:
        kvp_await(2, i, recv2.at[i])
    partials = [send2.at[me_m, me_c]] + [recv2.at[i] for i in range(nk - 1)]
    every = [p[32:48, :].astype(F32)[:8] for p in partials]
    every = jnp.concatenate(every + [jnp.zeros((8, HD), F32)] * (HD // 8 - nk), axis=0)
    turned = every.T[:32]
    joined = turned + pltpu.roll(turned, HD - 1, 1) + pltpu.roll(turned, HD - 2, 1)
    own_lane = (lane32 % 8 == 0) & (lane32 < 8 * nk)
    peak = jnp.max(jnp.where(own_lane, joined, FLOOR), axis=1, keepdims=True)
    peak = jnp.maximum(peak, draft_top)
    factor = jnp.where(own_lane, jnp.exp2((joined - peak) * EXP_SCALE), 0.0)
    whole = jnp.where(own_lane, factor * pltpu.roll(joined, HD - 3, 1), 0.0)
    draft_factor = jnp.exp2((draft_top - peak) * EXP_SCALE)
    whole = jnp.sum(whole, axis=1, keepdims=True) + draft_sum * draft_factor
    factor = factor / whole
    mixed = draft_out * (draft_factor / whole)
    for i in range(nk):
        mixed = mixed + partials[i][:32, :].astype(F32) * factor[:, 8 * i : 8 * i + 1]
    a0, a1, b0, b1 = mixed[:8], mixed[8:16], mixed[16:24], mixed[24:]
    h0, h1 = first_of(a0, b0), second_of(a0, b0)
    h2, h3 = first_of(a1, b1), second_of(a1, b1)
    gath2[me_m, me_c] = jnp.concatenate(
        [jnp.concatenate([h0, h1], axis=1), jnp.concatenate([h2, h3], axis=1)], axis=0
    ).astype(BF16)
    kvp_gather(3, gath2.at[me_m, me_c])
    finish()
    arrive(2)
    kvp_gather_wait(3, lambda source: gath2.at[source // 2, source % 2])

    heads = [
        jnp.concatenate([gath2[m, c].astype(F32)[8 * g : 8 * g + 8] for m in range(nm)], axis=0).astype(BF16)
        for c in range(2)
        for g in range(2)
    ]

    def attn_half(which):
        columns = pl.ds(pl.multiple_of(which * half, half), half)
        return sum(dot(heads[n], wo[256 * n : 256 * n + 256, columns]) for n in range(4))

    attn = head_sum(0, attn_half, core3, along3)
    resid[core] = (hidden_halves[core] + attn).astype(BF16)
    share_half(nz, resid)
    residual = jnp.concatenate([resid[0].astype(F32), resid[1].astype(F32)], axis=1)
    normed = (residual * post_ref[...].astype(F32).reshape(1, db)).astype(BF16)
    arrive(3)
    arrive(4)
    lines, direct = {}, []
    for p, (at, size, axis) in enumerate(pieces):
        part = pl.ds(at, size)
        for c in range(2):
            columns = slice(c * fh + at, c * fh + at + size)
            gate = dot(normed, wg[:, columns]).reshape(nm, 8, size)
            up = dot(normed, wu[:, columns]).reshape(nm, 8, size)
            both = jnp.concatenate([gate, up], axis=1).astype(BF16)
            send4[:, :, c, :, part] = both.reshape(side, side // 2, 16, size)
        if axis is None:
            direct.append((p, part))
            continue
        lines[p] = []
        for k in [side // 2] + [k for k in range(1, side) if k != side // 2]:
            if axis == "x":
                x = lax.rem(me_x + k, side)
                src, dst = send4.at[:, x // 2, x % 2, :, part], line_recv_x.at[k - 1, :, :, part]
            else:
                y = lax.rem(me_y + k, side)
                src, dst = send4.at[y, :, :, :, part], line_recv.at[k - 1, :, :, :, part]
            lines[p].append(line_copy(p, k, axis, src, dst))
        if p == 0:
            square_out = square_tile(jnp.sum(residual * residual, axis=1, keepdims=True)).reshape(nm, 8, HD)
            square_out = jnp.concatenate([square_out, jnp.zeros_like(square_out)], axis=1).astype(BF16)
            send_sq[:, 0] = square_out
            send_sq[:, 1] = square_out
            kvp_scatter(4, send_sq, recv_sq)
    for p, part in direct:
        for i, to in enumerate(targets):
            src = send4.at[to // side, (to % side) // 2, to % 2, :, part]
            kvp_start(5 + p, i, src, recv4.at[i, :, part])
    crossing = {}
    for p, (at, size, axis) in enumerate(pieces):
        if axis is None:
            continue
        part = pl.ds(at, size)
        for copy in lines[p]:
            copy.wait_recv()
        if axis == "x":
            own, here = send4[:, me_x // 2, me_x % 2, :, part], me_y
        else:
            own, here = send4[me_y, :, :, :, part].reshape(side, 16, size), me_x
        total = own.astype(F32)
        for k in range(1, side):
            if axis == "x":
                total = total + line_recv_x[k - 1, :, :, part].astype(F32)
            else:
                total = total + line_recv[k - 1, :, :, :, part].astype(F32).reshape(side, 16, size)
        line_sum[:, :, part] = total.astype(BF16)
        crossing[p] = [
            line_copy(
                2 + p,
                k,
                "y" if axis == "x" else "x",
                line_sum.at[lax.rem(here + k, side), :, part],
                cross_recv.at[k - 1, :, part],
            )
            for k in range(1, side)
        ]
    total = kvp_reduce(4, send_sq[me_m, me_c], recv_sq)
    inverse = lax.rsqrt(jnp.sum(total[:8], axis=1, keepdims=True) / width + EPSILON)
    base = 5 + len(pieces)
    order = [2, 0, 1]
    for p, (at, size, axis) in [(p, pieces[p]) for p in order]:
        part = pl.ds(at, size)
        if axis is None:
            own = send4[me_y, me_x // 2, me_c, :, part]
            total = kvp_reduce(5 + p, own, recv4.at[:, :, part])
        else:
            for copy in crossing[p]:
                copy.wait_recv()
            total = line_sum[me_y if axis == "x" else me_x, :, part].astype(F32)
            for k in range(1, side):
                total = total + cross_recv[k - 1, :, part].astype(F32)
        gate = total[:8] * inverse
        up = total[8:] * inverse
        middle = gate / (1.0 + jnp.exp(-gate)) * up
        mine = gath4.at[me_m, me_c, :, pl.ds(at // 2, size // 2)]
        mine[...] = folded(middle).astype(BF16)
        kvp_gather(base + p, mine)
    finish()
    arrive(5)
    down_part = jnp.zeros((rows, db), F32)
    for p, (at, size, _) in [(p, pieces[p]) for p in order]:
        part = pl.ds(at // 2, size // 2)
        kvp_gather_wait(base + p, lambda source, part=part: gath4.at[source // 2, source % 2, :, part])
        for c in range(2):
            rows_of = [gath4[m, c, :, part].astype(F32) for m in range(nm)]
            piece = jnp.concatenate(
                [jnp.concatenate([r[:8] for r in rows_of], axis=0), jnp.concatenate([r[8:] for r in rows_of], axis=0)],
                axis=1,
            ).astype(BF16)
            down_part += dot(piece, wd[c * fh + at : c * fh + at + size, :])
    down = head_sum(nz + 1, lambda which: jnp.where(which == 0, *halves(down_part)), core5, along5)
    final[core] = (resid[core].astype(F32) + down).astype(BF16)
    share_half(2 * nz + 1, final)
    next_ref[:, :half] = final[0]
    next_ref[:, half:] = final[1]
    finish()


def body(
    nk,
    nh,
    hidden_in,
    norm_gain,
    w_query,
    w_key,
    w_value,
    w_out,
    post_gain,
    w_gate,
    w_up,
    w_down,
    cache_keys,
    cache_values,
    context_len,
    slot_request,
    slot_start,
):
    rows, db = hidden_in.shape
    nm = nk // 2
    slots = cache_keys.shape[0]
    fh = w_gate.shape[1] // 2
    half, nz, side, count = db // 2, nh // 2, math.isqrt(nk), len(pieces_of(fh))
    exponent = np.arange(HD // 2, dtype=np.float32) * np.float32(2.0 / HD)
    frequency = (THETA_BASE ** (-exponent.astype(np.float64))).astype(np.float32)
    frequency = jnp.asarray(np.concatenate([frequency, frequency])[None, :])
    vmem = pl.BlockSpec(memory_space=pltpu.VMEM)
    hbm = pl.BlockSpec(memory_space=pl.ANY)
    scratch = [
        pltpu.VMEM(hidden_in.shape, BF16),
        pltpu.VMEM(norm_gain.shape, BF16),
        pltpu.VMEM(post_gain.shape, BF16),
        pltpu.VMEM(frequency.shape, F32),
        pltpu.SMEM(context_len.shape, jnp.int32),
        pltpu.SMEM(slot_request.shape, jnp.int32),
        pltpu.SMEM(slot_start.shape, jnp.int32),
    ]
    scratch += [
        pltpu.VMEM(w.shape, BF16)
        for w in (w_query, w_key, w_value, w_out, w_gate, w_up, w_down, cache_keys, cache_values)
    ]
    scratch += [
        pltpu.VMEM((2, rows, half), F32),
        pltpu.VMEM((nm, 2, 16, 384), BF16),
        pltpu.VMEM((nk - 1, 16, 384), BF16),
        pltpu.VMEM((nk, 2, 16, HD), BF16),
        pltpu.VMEM((nm, 2, 16, HD), BF16),
        pltpu.VMEM((slots // 2, HD, 2 * BLOCK), BF16),
        pltpu.VMEM((slots, 32, BLOCK), F32),
        pltpu.VMEM((slots, 32, BLOCK), F32),
        pltpu.VMEM((nk, 32, BLOCK), F32),
        pltpu.VMEM((slots, 32, HD), F32),
        pltpu.VMEM((slots, 32, BLOCK), F32),
        pltpu.VMEM((nm, 2, 48, HD), BF16),
        pltpu.VMEM((nk - 1, 48, HD), BF16),
        pltpu.VMEM((nm, 2, 16, 256), BF16),
        pltpu.VMEM((2, rows, half), BF16),
        pltpu.VMEM((nz, rows, half), BF16),
        pltpu.VMEM((2, rows, half), BF16),
        pltpu.VMEM((nm, 2, 16, HD), BF16),
        pltpu.VMEM((nk - 1, 16, HD), BF16),
        pltpu.VMEM((side, side // 2, 2, 16, fh), BF16),
        pltpu.VMEM((nk - 1, 16, fh), BF16),
        pltpu.VMEM((side - 1, side, 16, fh), BF16),
        pltpu.VMEM((side - 1, side // 2, 2, 16, fh), BF16),
        pltpu.VMEM((side, 16, fh), BF16),
        pltpu.VMEM((side - 1, 16, fh), BF16),
        pltpu.VMEM((nm, 2, 16, fh // 2), BF16),
        pltpu.VMEM((2, rows, half), BF16),
        pltpu.VMEM((nz, rows, half), BF16),
        pltpu.VMEM((2, rows, half), BF16),
        pltpu.SemaphoreType.DMA((16,)),
        pltpu.SemaphoreType.DMA((6 + 2 * count, nk)),
        pltpu.SemaphoreType.DMA((6 + 2 * count, nk)),
        pltpu.SemaphoreType.DMA((2 * nz + 2,)),
        pltpu.SemaphoreType.DMA((2 * nz + 2,)),
        pltpu.SemaphoreType.DMA((4, side)),
        pltpu.SemaphoreType.DMA((4, side)),
    ]
    weight_items = sum(w.size for w in (w_query, w_key, w_value, w_out, w_gate, w_up, w_down))
    results = pl.pallas_call(
        functools.partial(kernel, nk, nh, db * nk),
        out_shape=(
            jax.ShapeDtypeStruct((rows, db), BF16),
            jax.ShapeDtypeStruct((rows, HD), BF16),
            jax.ShapeDtypeStruct((rows, HD), BF16),
        ),
        in_specs=[hbm] * 16,
        out_specs=(vmem, vmem, vmem),
        scratch_shapes=scratch,
        compiler_params=pltpu.CompilerParams(
            collective_id=0, has_side_effects=True, vmem_limit_bytes=56 * 1024 * 1024
        ),
        cost_estimate=pl.CostEstimate(
            flops=2 * rows * weight_items + 4 * slots * 32 * BLOCK * HD,
            bytes_accessed=2 * (weight_items + 2 * cache_keys.size),
            transcendentals=slots * 32 * BLOCK,
        ),
    )(
        hidden_in,
        norm_gain,
        post_gain,
        frequency,
        w_query,
        w_key,
        w_value,
        w_out,
        w_gate,
        w_up,
        w_down,
        cache_keys,
        cache_values,
        context_len,
        slot_request,
        slot_start,
    )
    return pl.pallas_call(
        hand_on,
        out_shape=tuple(jax.ShapeDtypeStruct(r.shape, r.dtype) for r in results),
        in_specs=[vmem] * 3,
        out_specs=(vmem,) * 3,
    )(*results)


def solution(mesh):
    return jax.shard_map(
        functools.partial(body, mesh.shape["kvp"], mesh.shape["head"]),
        mesh=mesh,
        in_specs=(
            P(None, "kvp"),
            P("kvp"),
            P("kvp", "head"),
            P("kvp", "head"),
            P("kvp", "head"),
            P("head", "kvp"),
            P("kvp"),
            P("kvp", "head"),
            P("kvp", "head"),
            P("head", "kvp"),
            P("kvp", None, "head"),
            P("kvp", None, "head"),
            P(),
            P("kvp"),
            P("kvp"),
        ),
        out_specs=(P(None, "kvp"), P(None, "head"), P(None, "head")),
        check_vma=False,
    )
```
